128 devices in a mesh: section: 16 (over x, y), expert: 8 (over z, core).
Axes of the slice: x: 4, y: 4, z: 4, core: 2. Of those that a mesh axis runs over, the one named last changes fastest.
Arguments:
- tokens: bfloat16 [16384, 2048], P(('section', 'expert')), may hold values from -6 to 6
- w_gate: bfloat16 [8, 2048, 7168], P('expert', None, 'section'), may hold values from -0.125 to 0.125
- w_up: bfloat16 [8, 2048, 7168], P('expert', None, 'section'), may hold values from -0.125 to 0.125
- w_down: bfloat16 [8, 7168, 2048], P('expert', 'section'), may hold values from -0.0625 to 0.0625
- routes: int32 [16384, 2], P(('section', 'expert')), may hold values from 0 to 7, all different within a row; in each aligned block of 128 rows (0 to 127, 128 to 255, ...) at most 40 rows name the same one
- gates: float32 [16384, 2], P(('section', 'expert')), may hold values from 0.25 to 1
- document_index: int32 [16384], P(('section', 'expert')), may hold values from 0 to 15, as said below
- pool_mask: int32 [16384], P(('section', 'expert')), may hold values from 0 to 1, as said below
Outputs:
- moe_out: bfloat16 [16384, 2048], P(('section', 'expert'))
- embeddings: float32 [16, 2048], P(None, ('section', 'expert'))
- loss: float32 [], replicated
The draws below stay inside these ranges and needn't reach their ends.
Inputs may be any that keep to these rules, and one draw needn't show every extreme that they name: `routes`: each row names 2 different experts; among the rows of one device no expert is named more than 40 times, a bound that some block reaches. `document_index`: never falling along the tokens; every one of the 16 documents has 1 to 2048 tokens, one exactly 2048 and one exactly 1. `pool_mask`: the tokens of at least one document are all 0.
All inputs are finite; a program needn't handle non-finite values.
Results may differ from the reference program's by a relative error of at most 0.015.
Values may be sent and summed in bfloat16 or wider, within the bound.
No kernel may reach another device: no remote copies, remote signals or barrier semaphores. Data moves between devices by JAX's collectives and lax.ppermute only.
A program may use at most 128 MiB of HBM per device.

```python
import math
import jax
import jax.numpy as jnp
import numpy as np
from jax import lax

D = 2048
FF = 7168
TOP = 2
TOK_DEV = 128
DOC_LEN = 2048
EXPERTS = 8
TOKENS = 16384
CAP = 40
PAIRS = 8
DOCS = 16
N_SECTION = 16
N_EXPERT = 8


def doc_layout(key):
    key_pairs = jax.random.fold_in(key, 101)
    key_second = jax.random.fold_in(key, 102)
    key_order = jax.random.fold_in(key, 103)
    pair_len = jax.random.randint(key_pairs, (PAIRS,), 1, DOC_LEN, dtype=jnp.int32)
    second_len = jax.random.randint(key_second, (), 1, DOC_LEN - 1, dtype=jnp.int32)
    special = jnp.stack([jnp.ones((), jnp.int32), second_len, jnp.full((), DOC_LEN, jnp.int32), (DOC_LEN - 1 - second_len).astype(jnp.int32)])
    remainder = jnp.stack([pair_len, (DOC_LEN - pair_len).astype(jnp.int32)], axis=1).reshape(-1)[4:]
    lengths = jnp.concatenate([special, remainder]).astype(jnp.int32)
    shuffle = jax.random.permutation(key_order, DOCS).astype(jnp.int32)
    lengths = lengths[shuffle]
    tiny_doc = jnp.argmax((shuffle == 0).astype(jnp.int32)).astype(jnp.int32)
    doc_ends = jnp.cumsum(lengths).astype(jnp.int32)
    positions = jnp.arange(TOKENS, dtype=jnp.int32)
    doc_ids = jnp.sum((positions[:, None] >= doc_ends[None, :]).astype(jnp.int32), axis=1).astype(jnp.int32)
    return (doc_ids, tiny_doc)


def draw_document_index(key, part):
    doc_ids, tiny_doc = doc_layout(key)
    return doc_ids


def draw_pool_mask(key, part):
    doc_ids, tiny_doc = doc_layout(key)
    key = jax.random.fold_in(key, 12)
    chance = jax.random.randint(key, (TOKENS,), 0, 4, dtype=jnp.int32)
    pooled = (chance < 3).astype(jnp.int32)
    return jnp.where(doc_ids == tiny_doc, 0, pooled).astype(jnp.int32)


def block_levels(own_key, shape, cuts, least, high):
    def one(dim, parts):
        heights = jax.random.uniform(jax.random.fold_in(jax.random.fold_in(own_key, 6), dim), (parts,), jnp.float32, least / len(cuts), high / len(cuts))
        return jnp.repeat(jnp.exp(heights), shape[dim] // parts).reshape((-1,) + (1,) * (len(shape) - dim - 1))

    factor_of = one(*cuts[0])
    for cut in cuts[1:]:
        factor_of = factor_of * one(*cut)
    return factor_of


def shared_out(key, own, number, rows, number_of, top, reach, lean):
    sequence = jax.random.permutation(key, number_of)
    crowded, ordinary = shares(number_of, rows * top, reach, lean, True), shares(number_of, rows * top, reach, lean, False)
    places = jnp.arange(number_of)

    def named(tallies, offset_by):
        used = int((tallies > 0).sum())
        fixed = max(1, used // 4)
        moved = fixed + (places - fixed + offset_by * (used - fixed)) % max(1, number_of - fixed)
        return jnp.zeros((number_of,), jnp.int32).at[sequence[jnp.where(places < fixed, places, moved)]].set(jnp.asarray(tallies, jnp.int32))

    tallies = jnp.where(number % 4 == 0, named(crowded, number // 4), named(ordinary, number - number // 4 - 1))
    mixed = jax.random.permutation(jax.random.fold_in(own, 3), number_of)
    source_of, receiver = mixed[0:number_of // 2 * 2:2], mixed[1:number_of // 2 * 2:2]
    room = jnp.minimum(tallies[source_of] - 1, reach - tallies[receiver]) // 2
    room = jnp.where((source_of == sequence[0]) | (receiver == sequence[0]) | (tallies[receiver] == 0), 0, jnp.maximum(room, 0))
    moved = jax.random.randint(jax.random.fold_in(own, 4), (number_of // 2,), 0, 1 << 20) % (room + 1)
    tallies = tallies.at[source_of].add(-moved).at[receiver].add(moved)
    labels = jnp.searchsorted(jnp.cumsum(tallies), jnp.arange(rows * top), side="right").astype(jnp.int32)
    table = labels.reshape(top, rows).T
    table = table[jax.random.permutation(jax.random.fold_in(own, 1), rows)]
    offset_by = jax.random.randint(jax.random.fold_in(own, 2), (rows, 1), 0, top)
    return jnp.take_along_axis(table, (jnp.arange(top)[None, :] + offset_by) % top, axis=1)


def shares(amount, total, limit, slope, full):
    weights = [(1 << 20) // math.isqrt(rank ** slope) + 1 for rank in range(1, amount + 1)]
    largest = limit if full else min(limit, max(-(-total // amount), total * weights[0] // sum(weights)))
    least = 1 if total - largest >= amount - 1 else 0
    holding, rest = [largest] + [least] * (amount - 1), total - largest - least * (amount - 1)
    while rest > 0:
        movable = [i for i in range(1, amount) if holding[i] < largest] or [i for i in range(1, amount) if holding[i] < limit]
        mass, budget = sum([weights[i] for i in movable]), rest
        for i in movable:
            extra = min(limit - holding[i], max(1, budget * weights[i] // mass), rest)
            holding[i] = holding[i] + extra
            rest = rest - extra
    return np.array(holding)


def centred(stream_key, dims, width, most, pieces=(), kind=jnp.bfloat16):
    array = width * jax.random.normal(stream_key, dims, jnp.float32)
    if pieces:
        array = array * block_levels(stream_key, dims, pieces, -0.22, 0.18)
    return jnp.clip(array, -most, most).astype(kind)


def setup_inputs(seed: int = 0) -> dict:
    key_list = jax.random.split(jax.random.key(seed), 9)
    tokens = centred(key_list[0], (TOKENS, D), 1.0, 6.0, ((0, 128),))
    w_gate = centred(key_list[1], (EXPERTS, D, FF), D ** -0.5, 0.125, ((0, 8), (2, 16)))
    w_up = centred(key_list[2], (EXPERTS, D, FF), D ** -0.5, 0.125, ((0, 8), (2, 16)))
    w_down = centred(key_list[3], (EXPERTS, FF, D), FF ** -0.5, 0.0625, ((0, 8), (1, 16)))
    routes_keys = jax.random.split(jax.random.fold_in(key_list[4], 1), TOKENS // TOK_DEV)
    routes_turns = jax.random.permutation(jax.random.fold_in(key_list[4], 3), TOKENS // TOK_DEV)
    routes = jax.vmap(lambda own, number: shared_out(jax.random.fold_in(key_list[4], 2), own, number, TOK_DEV, EXPERTS, TOP, CAP, 1))(routes_keys, routes_turns).reshape((TOKENS, TOP))
    gates = jnp.clip(0.25 + 0.75 * jax.random.uniform(key_list[5], (TOKENS, TOP), jnp.float32) ** block_levels(key_list[5], (TOKENS, TOP), ((0, 128),), -0.2, 0.2), 0.25, 1.0)
    document_index = draw_document_index(jax.random.fold_in(key_list[8], 71), 0)
    pool_mask = draw_pool_mask(jax.random.fold_in(key_list[8], 71), 0)
    return {"tokens": tokens, "w_gate": w_gate, "w_up": w_up, "w_down": w_down, "routes": routes, "gates": gates, "document_index": document_index, "pool_mask": pool_mask}


SOFTMAX_TEMPER = 0.05

def contrast(squares_q, squares_p, cross_entropy_term, feature_total):
    query_scale = lax.rsqrt(squares_q / feature_total + 1e-06)
    passage_scale = lax.rsqrt(squares_p / feature_total + 1e-06)
    similarity_matrix = cross_entropy_term * query_scale[:, None] * passage_scale[None, :] / (feature_total * SOFTMAX_TEMPER)
    return jnp.mean(jnp.log(lax.optimization_barrier(jnp.sum(jnp.exp(similarity_matrix), axis=1))) - jnp.diagonal(similarity_matrix))

def reference(tokens, w_gate, w_up, w_down, routes, gates, document_index, pool_mask):
    bound = N_SECTION * N_EXPERT * CAP
    group_width = FF // N_SECTION

    def one_expert(expert):
        named = routes == expert
        hit = jnp.any(named, axis=1)
        order = jnp.argsort(jnp.where(hit, 0, 1).astype(jnp.int32), stable=True)[:bound].astype(jnp.int32)
        picked = tokens[order]
        weight = lax.optimization_barrier(jnp.sum(jnp.where(named, gates, 0.0), axis=1))[order]
        gate_act = jnp.dot(picked, w_gate[expert], preferred_element_type=jnp.float32)
        up_act = jnp.dot(picked, w_up[expert], preferred_element_type=jnp.float32)
        hidden = (jax.nn.silu(gate_act) * up_act).astype(jnp.bfloat16)
        total = jnp.zeros((bound, D), jnp.float32)
        for group in range(N_SECTION):
            term = jnp.dot(hidden[:, group * group_width:(group + 1) * group_width], w_down[expert, group * group_width:(group + 1) * group_width], preferred_element_type=jnp.float32)
            term = lax.optimization_barrier(term.astype(jnp.bfloat16))
            total = total + term.astype(jnp.float32)
        expert_out = total.astype(jnp.bfloat16)
        return (order, weight[:, None] * expert_out.astype(jnp.float32))
    orders, weighted = lax.map(one_expert, jnp.arange(EXPERTS, dtype=jnp.int32))
    combined = jnp.zeros((TOKENS, D), jnp.float32).at[orders.reshape(-1)].add(weighted.reshape(-1, D))
    moe_out = (tokens.astype(jnp.float32) + combined).astype(jnp.bfloat16)
    member = (document_index[:, None] == jnp.arange(DOCS, dtype=jnp.int32)[None, :]) & (pool_mask[:, None] == 1)
    member = member.astype(jnp.bfloat16)
    sums = jnp.dot(member.T, moe_out, preferred_element_type=jnp.float32)
    counts = lax.optimization_barrier(jnp.sum(member.astype(jnp.float32), axis=0))
    embeddings = sums / jnp.maximum(counts, 1.0)[:, None]
    queries = embeddings[0::2]
    passages = embeddings[1::2]
    cross_entropy_term = jnp.dot(queries, passages.T, precision=lax.Precision.HIGHEST)
    loss = contrast(lax.optimization_barrier(jnp.sum(queries * queries, axis=1)), lax.optimization_barrier(jnp.sum(passages * passages, axis=1)), cross_entropy_term, D)
    return (moe_out, embeddings, loss)
```

```python
import math

import jax
import jax.numpy as jnp
from jax import lax
from jax.sharding import PartitionSpec as P

SOFTMAX_TEMPER = 0.05
AXES = ("section", "expert")
DOC_LEN = 2048
LANES = 128


def contrast(squares_q, squares_p, cross_entropy_term, feature_total):
    query_scale = lax.rsqrt(squares_q / feature_total + 1e-06)
    passage_scale = lax.rsqrt(squares_p / feature_total + 1e-06)
    similarity_matrix = (
        cross_entropy_term
        * query_scale[:, None]
        * passage_scale[None, :]
        / (feature_total * SOFTMAX_TEMPER)
    )
    eye = jnp.eye(similarity_matrix.shape[0], dtype=jnp.float32)
    return jnp.mean(
        jnp.log(jnp.sum(jnp.exp(similarity_matrix), axis=1))
        - jnp.sum(similarity_matrix * eye, axis=1)
    )


def slot_table(block_routes, expert_count, capacity):
    tok_count, choose = block_routes.shape
    flat_routes = block_routes.reshape(-1)
    chosen = (flat_routes[:, None] == jnp.arange(expert_count, dtype=jnp.int32)[None, :]).astype(
        jnp.int32
    )
    position = jnp.sum((jnp.cumsum(chosen, axis=0) - 1) * chosen, axis=1)
    target = flat_routes * capacity + position
    placing = target[:, None] == jnp.arange(expert_count * capacity, dtype=jnp.int32)[None, :]
    return placing.reshape(tok_count, choose, expert_count * capacity)


def permutation(side, depth, axis_of_core, step):
    pairs = []
    for x in range(side):
        for y in range(side):
            for z in range(depth):
                for core in range(2):
                    to = ((x + step) % side, y) if axis_of_core[core] == 0 else (x, (y + step) % side)
                    here = ((x * side + y) * depth + z) * 2 + core
                    there = ((to[0] * side + to[1]) * depth + z) * 2 + core
                    pairs.append((here, there))
    return pairs


def z_permutation(side, depth, step):
    return [
        ((s * depth + z) * 2 + c, (s * depth + (z + step) % depth) * 2 + c)
        for s in range(side * side)
        for z in range(depth)
        for c in range(2)
    ]


def shards(tokens, w_gate, w_up, w_down, routes, gates, document_index, pool_mask):
    tok_count, feature_total = tokens.shape
    choose = routes.shape[1]
    expert_count = lax.axis_size("expert")
    section_count = lax.axis_size("section")
    side = math.isqrt(section_count)
    depth = expert_count // 2
    capacity = tok_count * choose * 5 // (4 * expert_count)
    slots = expert_count * capacity
    device_count = section_count * expert_count
    doc_count = 2 * (tok_count * device_count // DOC_LEN)
    hidden_width = w_gate.shape[2]
    half_features = feature_total // 2
    half_slots = slots // 2

    def by_weight(a, step):
        return lax.ppermute(a, AXES, permutation(side, depth, (0, 1), step))

    def by_token(a, step):
        return lax.ppermute(a, AXES, permutation(side, depth, (1, 0), step))

    down = w_down[0]
    down_p, down_m = by_weight(down, 1), by_weight(down, -1)
    both = jnp.concatenate([w_gate[0], w_up[0]], axis=1)
    both_p, both_m = by_weight(both, 1), by_weight(both, -1)
    both_far = jnp.concatenate(
        [by_weight(both_p[:half_features], 1), by_weight(both_m[half_features:], -1)], axis=0
    )
    down_far_a = by_weight(down_p[:, :half_features], 1)
    down_far_b = by_weight(down_m[:, half_features:], -1)

    placing = slot_table(routes, expert_count, capacity)
    weighting = jnp.sum(jnp.where(placing, gates[:, :, None], 0.0), axis=1)
    member = (document_index[:, None] == jnp.arange(doc_count, dtype=jnp.int32)[None, :]) & (
        pool_mask[:, None] == 1
    )
    select = jnp.any(placing, axis=1).astype(jnp.bfloat16)
    filled = jnp.dot(select.T, tokens, preferred_element_type=jnp.float32).astype(jnp.bfloat16)
    shares = jnp.dot(
        weighting.T, member.astype(jnp.float32), precision=lax.Precision.HIGHEST
    )
    high = lax.reduce_precision(shares, 8, 7)
    extra = jnp.concatenate(
        [
            high.astype(jnp.bfloat16),
            (shares - high).astype(jnp.bfloat16),
            jnp.zeros((slots, LANES - 2 * doc_count), jnp.bfloat16),
        ],
        axis=1,
    )
    filled = jnp.concatenate([filled, extra], axis=1)
    mine = lax.all_to_all(
        filled.reshape(expert_count, capacity, -1), "expert", split_axis=0, concat_axis=0, tiled=True
    ).reshape(slots, -1)
    token_p, token_m = by_token(mine, 1), by_token(mine, -1)
    token_far_a = by_token(token_p[:half_slots], 1)
    token_far_b = by_token(token_m[half_slots:], -1)
    rows_all = jnp.concatenate([mine, token_p, token_m, token_far_a, token_far_b], axis=0)
    rows = rows_all[:, :feature_total]
    row_shares = rows_all[:, feature_total : feature_total + 2 * doc_count]

    def hidden_of(weights):
        act = jnp.dot(rows, weights, preferred_element_type=jnp.float32)
        return (jax.nn.silu(act[:, :hidden_width]) * act[:, hidden_width:]).astype(jnp.bfloat16)

    near = jnp.concatenate([hidden_of(both), hidden_of(both_p), hidden_of(both_m)], axis=1)
    near_out = jnp.dot(
        near, jnp.concatenate([down, down_p, down_m], axis=0), preferred_element_type=jnp.float32
    )
    far = hidden_of(both_far)
    far_out = jnp.concatenate(
        [
            jnp.dot(far, down_far_a, preferred_element_type=jnp.float32),
            jnp.dot(far, down_far_b, preferred_element_type=jnp.float32),
        ],
        axis=1,
    )
    partial = (near_out + far_out).astype(jnp.bfloat16)

    out_own, out_p, out_m, out_far = jnp.split(partial, 4, axis=0)
    far_a = by_token(out_far[:half_slots], -1)
    far_b = by_token(out_far[half_slots:], 1)
    from_m_b = by_token(out_p[half_slots:], -1)
    from_p_a = by_token(out_m[:half_slots], 1)
    from_m_a = by_token(
        (out_p[:half_slots].astype(jnp.float32) + far_a.astype(jnp.float32)).astype(jnp.bfloat16), -1
    )
    from_p_b = by_token(
        (out_m[half_slots:].astype(jnp.float32) + far_b.astype(jnp.float32)).astype(jnp.bfloat16), 1
    )
    expert_out = (
        out_own.astype(jnp.float32)
        + jnp.concatenate([from_m_a, from_m_b], axis=0).astype(jnp.float32)
        + jnp.concatenate([from_p_a, from_p_b], axis=0).astype(jnp.float32)
    ).astype(jnp.bfloat16)
    returned = lax.all_to_all(
        expert_out.reshape(expert_count, capacity, feature_total),
        "expert",
        split_axis=0,
        concat_axis=0,
        tiled=True,
    )
    combined = jnp.dot(
        weighting,
        returned.reshape(slots, feature_total).astype(jnp.float32),
        precision=lax.Precision.HIGHEST,
    )
    moe_out = (tokens.astype(jnp.float32) + combined).astype(jnp.bfloat16)

    member_bf = member.astype(jnp.bfloat16)
    pooled = jnp.dot(row_shares.T, partial, preferred_element_type=jnp.float32)
    sums = (
        pooled[:doc_count]
        + pooled[doc_count:]
        + jnp.dot(member_bf.T, tokens, preferred_element_type=jnp.float32)
    )
    counts = jnp.sum(member.astype(jnp.float32), axis=0)
    total = jnp.concatenate(
        [sums, jnp.broadcast_to(counts[:, None], (doc_count, LANES))], axis=1
    )
    flip = [(i, i ^ 1) for i in range(device_count)]
    total = total + lax.ppermute(total, AXES, flip)
    for pairs_of in (
        lambda step: z_permutation(side, depth, step),
        lambda step: permutation(side, depth, (1, 0), step),
        lambda step: permutation(side, depth, (0, 1), step),
    ):
        one, two, three = (lax.ppermute(total, AXES, pairs_of(step)) for step in (1, 2, 3))
        total = (total + two) + (one + three)
    embeddings = total[:, :feature_total] / jnp.maximum(total[:, feature_total:][:, :1], 1.0)
    queries = embeddings[0::2]
    passages = embeddings[1::2]
    cross_entropy_term = jnp.dot(queries, passages.T, precision=lax.Precision.HIGHEST)
    loss = contrast(
        jnp.sum(queries * queries, axis=1),
        jnp.sum(passages * passages, axis=1),
        cross_entropy_term,
        feature_total,
    )
    share = feature_total // device_count
    emb_share = lax.dynamic_slice_in_dim(embeddings, lax.axis_index(AXES) * share, share, 1)
    return (moe_out, emb_share, loss)


def solution(mesh):
    return jax.shard_map(
        shards,
        mesh=mesh,
        in_specs=(
            P(("section", "expert"), None),
            P("expert", None, "section"),
            P("expert", None, "section"),
            P("expert", "section", None),
            P(("section", "expert"), None),
            P(("section", "expert"), None),
            P(("section", "expert")),
            P(("section", "expert")),
        ),
        out_specs=(P(("section", "expert"), None), P(None, ("section", "expert")), P()),
        check_vma=False,
    )
```

```python
import math

import jax
import jax.numpy as jnp
from jax import lax
from jax.experimental import pallas as pl
from jax.experimental.pallas import tpu as pltpu
from jax.sharding import PartitionSpec as P

SOFTMAX_TEMPER = 0.05
AXES = ("section", "expert")
DOC_LEN = 2048
LANES = 128


def contrast(squares_q, squares_p, cross_entropy_term, feature_total):
    query_scale = lax.rsqrt(squares_q / feature_total + 1e-06)
    passage_scale = lax.rsqrt(squares_p / feature_total + 1e-06)
    similarity_matrix = (
        cross_entropy_term
        * query_scale[:, None]
        * passage_scale[None, :]
        / (feature_total * SOFTMAX_TEMPER)
    )
    eye = jnp.eye(similarity_matrix.shape[0], dtype=jnp.float32)
    return jnp.mean(
        jnp.log(jnp.sum(jnp.exp(similarity_matrix), axis=1))
        - jnp.sum(similarity_matrix * eye, axis=1)
    )


def slot_table(block_routes, expert_count, capacity):
    tok_count, choose = block_routes.shape
    flat_routes = block_routes.reshape(-1)
    chosen = (flat_routes[:, None] == jnp.arange(expert_count, dtype=jnp.int32)[None, :]).astype(
        jnp.int32
    )
    position = jnp.sum((jnp.cumsum(chosen, axis=0) - 1) * chosen, axis=1)
    target = flat_routes * capacity + position
    placing = target[:, None] == jnp.arange(expert_count * capacity, dtype=jnp.int32)[None, :]
    return placing.reshape(tok_count, choose, expert_count * capacity)


def permutation(side, depth, axis_of_core, step):
    pairs = []
    for x in range(side):
        for y in range(side):
            for z in range(depth):
                for core in range(2):
                    to = ((x + step) % side, y) if axis_of_core[core] == 0 else (x, (y + step) % side)
                    here = ((x * side + y) * depth + z) * 2 + core
                    there = ((to[0] * side + to[1]) * depth + z) * 2 + core
                    pairs.append((here, there))
    return pairs


def z_permutation(side, depth, step):
    return [
        ((s * depth + z) * 2 + c, (s * depth + (z + step) % depth) * 2 + c)
        for s in range(side * side)
        for z in range(depth)
        for c in range(2)
    ]


def after(value, *earlier):
    return lax.optimization_barrier((value,) + earlier)[0]


def experts_kernel(parts, last, first_block, half_rows, *refs):
    weight_count = 1 + max(max(part[0], part[2], part[4]) for part in parts)
    x_ref, refs = refs[0], refs[1:]
    weights, refs = refs[:weight_count], refs[weight_count:]
    if first_block:
        acc_ref = None
    else:
        acc_ref, refs = refs[0], refs[1:]
    if last == "rest":
        base_ref, refs = refs[0], refs[1:]
    outs, sums_ref, pooled = refs[:-2], refs[-2], refs[-1]
    step, steps = pl.program_id(0), pl.num_programs(0)
    features = weights[0].shape[1]
    x = x_ref[:, :features]
    shares = x_ref[:, features:]
    nt = (((1,), (1,)), ((), ()))
    tn = (((0,), (0,)), ((), ()))

    @pl.when(step == 0)
    def _():
        pooled[...] = jnp.zeros_like(pooled)

    total = None if acc_ref is None else acc_ref[...]
    for at, (g, g_row, u, u_row, d, d_row, width) in enumerate(parts):
        gate = lax.dot_general(
            x, weights[g][g_row : g_row + width, :], nt, preferred_element_type=jnp.float32
        )
        up = lax.dot_general(
            x, weights[u][u_row : u_row + width, :], nt, preferred_element_type=jnp.float32
        )
        hidden = (gate / (1.0 + jnp.exp(-gate)) * up).astype(jnp.bfloat16)
        pooled[at] += lax.dot_general(shares, hidden, tn, preferred_element_type=jnp.float32)
        out = jnp.dot(
            hidden, weights[d][d_row : d_row + width, :], preferred_element_type=jnp.float32
        )
        total = out if total is None else total + out
    if last is None:
        outs[0][...] = total
    elif last == "far":
        outs[0][...] = total[:half_rows].astype(jnp.bfloat16)
        outs[1][...] = total[half_rows:].astype(jnp.bfloat16)
    else:
        @pl.when(step == 0)
        def _():
            outs[1][...] = total[:half_rows].astype(jnp.bfloat16)
            outs[2][...] = total[half_rows:].astype(jnp.bfloat16)

        @pl.when(step == 1)
        def _():
            outs[3][...] = total[:half_rows].astype(jnp.bfloat16)
            outs[4][...] = total[half_rows:].astype(jnp.bfloat16)

        @pl.when(step == 2)
        def _():
            outs[0][...] = total.astype(jnp.bfloat16)

    @pl.when(step == steps - 1)
    def _():
        docs = sums_ref.shape[0]
        sums = jnp.zeros((docs, features), jnp.float32)
        for at, (_, _, _, _, d, d_row, width) in enumerate(parts):
            both = pooled[at][:docs] + pooled[at][docs : 2 * docs]
            high = both.astype(jnp.bfloat16)
            low = (both - high.astype(jnp.float32)).astype(jnp.bfloat16)
            down = weights[d][d_row : d_row + width, :]
            sums += jnp.dot(high, down, preferred_element_type=jnp.float32)
            sums += jnp.dot(low, down, preferred_element_type=jnp.float32)
        if last == "rest":
            sums_ref[:, :features] = sums + base_ref[:, :features]
            sums_ref[:, features:] = base_ref[:, features:]
        else:
            sums_ref[...] = sums


def run_experts(rows, weights, parts, acc, block, order, last, docs, base=None):
    features = weights[0].shape[1]
    wide = rows.shape[1]
    steps = len(order)
    if steps == 1:
        place = lambda i: (order[0], 0)
    elif order == (1, 2, 0):
        place = lambda i: (lax.rem(i + 1, 3), 0)
    else:
        place = lambda i: (i, 0)
    whole = lambda shape: pl.BlockSpec(shape, lambda i: (0, 0), pipeline_mode=pl.Buffered(1))
    in_specs = [pl.BlockSpec((block, wide), place)]
    in_specs += [whole(w.shape) for w in weights]
    operands = [rows, *weights]
    aliases = {}
    if acc is not None:
        in_specs.append(pl.BlockSpec((block, features), place))
        operands.append(acc)
        if last is None:
            aliases = {len(operands) - 1: 0}
    if base is not None:
        in_specs.append(whole(base.shape))
        operands.append(base)
    half = block // 2
    if last is None:
        out_shape = [jax.ShapeDtypeStruct((rows.shape[0], features), jnp.float32)]
        out_specs = [pl.BlockSpec((block, features), place)]
    else:
        shapes = [half, half] if last == "far" else [block] + [half] * 4
        out_shape = [jax.ShapeDtypeStruct((n, features), jnp.bfloat16) for n in shapes]
        out_specs = [whole((n, features)) for n in shapes]
    sums_wide = features if base is None else base.shape[1]
    out_shape.append(jax.ShapeDtypeStruct((docs, sums_wide), jnp.float32))
    out_specs.append(whole((docs, sums_wide)))
    width = parts[0][-1]
    hidden = sum(part[-1] for part in parts)
    flops = 6 * steps * block * features * hidden
    return pl.pallas_call(
        lambda *refs: experts_kernel(parts, last, acc is None, half, *refs),
        grid=(steps,),
        in_specs=in_specs,
        out_specs=out_specs,
        out_shape=out_shape,
        scratch_shapes=[pltpu.VMEM((len(parts), wide - features, width), jnp.float32)],
        input_output_aliases=aliases,
        compiler_params=pltpu.CompilerParams(vmem_limit_bytes=44 * 1024 * 1024),
        cost_estimate=pl.CostEstimate(
            flops=flops,
            bytes_accessed=6 * hidden * features + steps * block * features * 10,
            transcendentals=steps * block * hidden,
        ),
    )(*operands)


def shards(tokens, w_gate, w_up, w_down, routes, gates, document_index, pool_mask):
    tok_count, feature_total = tokens.shape
    choose = routes.shape[1]
    expert_count = lax.axis_size("expert")
    section_count = lax.axis_size("section")
    side = math.isqrt(section_count)
    depth = expert_count // 2
    capacity = tok_count * choose * 5 // (4 * expert_count)
    slots = expert_count * capacity
    device_count = section_count * expert_count
    doc_count = 2 * (tok_count * device_count // DOC_LEN)
    half_hidden = w_gate.shape[2] // 2
    half_slots = slots // 2

    def by_weight(a, step):
        return lax.ppermute(a, AXES, permutation(side, depth, (0, 1), step))

    def by_token(a, step):
        return lax.ppermute(a, AXES, permutation(side, depth, (1, 0), step))

    gate, up, down = w_gate[0].T, w_up[0].T, w_down[0]
    gate_a, gate_b = gate[:half_hidden], gate[half_hidden:]
    gate_a_p, gate_a_m = by_weight(gate_a, 1), by_weight(gate_a, -1)
    gate_b_p, gate_b_m = by_weight(gate_b, 1), by_weight(gate_b, -1)

    placing = slot_table(routes, expert_count, capacity)
    weighting = jnp.sum(jnp.where(placing, gates[:, :, None], 0.0), axis=1)
    member = (document_index[:, None] == jnp.arange(doc_count, dtype=jnp.int32)[None, :]) & (
        pool_mask[:, None] == 1
    )
    select = jnp.any(placing, axis=1).astype(jnp.bfloat16)
    filled = jnp.dot(select.T, tokens, preferred_element_type=jnp.float32).astype(jnp.bfloat16)
    shares = jnp.dot(
        weighting.T, member.astype(jnp.float32), precision=lax.Precision.HIGHEST
    )
    high = lax.reduce_precision(shares, 8, 7)
    extra = jnp.concatenate(
        [
            high.astype(jnp.bfloat16),
            (shares - high).astype(jnp.bfloat16),
            jnp.zeros((slots, LANES - 2 * doc_count), jnp.bfloat16),
        ],
        axis=1,
    )
    filled = jnp.concatenate([filled, extra], axis=1)
    filled = after(filled, gate_a_p, gate_a_m)
    mine = lax.all_to_all(
        filled.reshape(expert_count, capacity, -1), "expert", split_axis=0, concat_axis=0, tiled=True
    ).reshape(slots, -1)
    up = after(up, gate_a_p, gate_a_m)
    up_p, up_m = by_weight(up, 1), by_weight(up, -1)
    down_late = after(down, gate_b_p, gate_b_m)
    down_p, down_m = by_weight(down_late, 1), by_weight(down_late, -1)
    token_p, token_m = by_token(mine, 1), by_token(mine, -1)
    token_far_a = by_token(token_p[:half_slots], 1)
    token_far_b = by_token(token_m[half_slots:], -1)
    gate_far_a = by_weight(after(gate_a_p, token_p, token_m), 1)
    gate_far_b = by_weight(after(gate_b_m, token_p, token_m), -1)
    up_far_a = by_weight(after(up_p[:half_hidden], token_p, token_m), 1)
    up_far_b = by_weight(after(up_m[half_hidden:], token_p, token_m), -1)
    down_far_a = by_weight(down_p[:half_hidden], 1)
    down_far_b = by_weight(down_m[half_hidden:], -1)
    rows = jnp.concatenate([mine, token_p, token_m, token_far_a, token_far_b], axis=0)

    member_bf = member.astype(jnp.bfloat16)
    token_sums = jnp.dot(member_bf.T, tokens, preferred_element_type=jnp.float32)
    counts = jnp.sum(member.astype(jnp.float32), axis=0)

    h = half_hidden
    everything = (0, 1, 2, 3)
    acc, sums_own = run_experts(
        rows,
        [gate, w_up[0].T, down],
        [(0, 0, 1, 0, 2, 0, h), (0, h, 1, h, 2, h, h)],
        None,
        slots,
        everything,
        None,
        doc_count,
    )
    acc, sums_near = run_experts(
        rows,
        [gate_a_p, gate_b_p, up_p, down_p, gate_a_m, gate_b_m, up_m, down_m],
        [
            (0, 0, 2, 0, 3, 0, h),
            (1, 0, 2, h, 3, h, h),
            (4, 0, 6, 0, 7, 0, h),
            (5, 0, 6, h, 7, h, h),
        ],
        acc,
        slots,
        everything,
        None,
        doc_count,
    )
    base = jnp.concatenate(
        [
            token_sums + sums_own + sums_near,
            jnp.broadcast_to(counts[:, None], (doc_count, LANES)),
        ],
        axis=1,
    )
    far_weights = [gate_far_a, gate_far_b, up_far_a, up_far_b, down_far_a, down_far_b]
    far_parts = [(0, 0, 2, 0, 4, 0, h), (1, 0, 3, 0, 5, 0, h)]
    out_far_a, out_far_b, sums_far = run_experts(
        rows, far_weights, far_parts, acc, slots, (3,), "far", doc_count
    )
    far_a = by_token(out_far_a, -1)
    far_b = by_token(out_far_b, 1)
    base = jnp.concatenate([base[:, :feature_total] + sums_far, base[:, feature_total:]], axis=1)
    out_own, out_p_a, out_p_b, out_m_a, out_m_b, total = run_experts(
        rows, far_weights, far_parts, acc, slots, (1, 2, 0), "rest", doc_count, base
    )

    from_m_b = by_token(out_p_b, -1)
    from_p_a = by_token(out_m_a, 1)
    from_m_a = by_token(
        (out_p_a.astype(jnp.float32) + far_a.astype(jnp.float32)).astype(jnp.bfloat16), -1
    )
    from_p_b = by_token(
        (out_m_b.astype(jnp.float32) + far_b.astype(jnp.float32)).astype(jnp.bfloat16), 1
    )
    expert_out = (
        out_own.astype(jnp.float32)
        + jnp.concatenate([from_m_a, from_m_b], axis=0).astype(jnp.float32)
        + jnp.concatenate([from_p_a, from_p_b], axis=0).astype(jnp.float32)
    ).astype(jnp.bfloat16)
    returned = lax.all_to_all(
        expert_out.reshape(expert_count, capacity, feature_total),
        "expert",
        split_axis=0,
        concat_axis=0,
        tiled=True,
    )
    combined = jnp.dot(
        weighting,
        returned.reshape(slots, feature_total).astype(jnp.float32),
        precision=lax.Precision.HIGHEST,
    )
    moe_out = (tokens.astype(jnp.float32) + combined).astype(jnp.bfloat16)

    flip = [(i, i ^ 1) for i in range(device_count)]
    total = total + lax.ppermute(total, AXES, flip)
    for pairs_of in (
        lambda step: z_permutation(side, depth, step),
        lambda step: permutation(side, depth, (1, 0), step),
        lambda step: permutation(side, depth, (0, 1), step),
    ):
        one, two, three = (lax.ppermute(total, AXES, pairs_of(step)) for step in (1, 2, 3))
        total = (total + two) + (one + three)
    embeddings = total[:, :feature_total] / jnp.maximum(total[:, feature_total:][:, :1], 1.0)
    queries = embeddings[0::2]
    passages = embeddings[1::2]
    cross_entropy_term = jnp.dot(queries, passages.T, precision=lax.Precision.HIGHEST)
    loss = contrast(
        jnp.sum(queries * queries, axis=1),
        jnp.sum(passages * passages, axis=1),
        cross_entropy_term,
        feature_total,
    )
    share = feature_total // device_count
    emb_share = lax.dynamic_slice_in_dim(embeddings, lax.axis_index(AXES) * share, share, 1)
    return (moe_out, emb_share, loss)


def solution(mesh):
    return jax.shard_map(
        shards,
        mesh=mesh,
        in_specs=(
            P(("section", "expert"), None),
            P("expert", None, "section"),
            P("expert", None, "section"),
            P("expert", "section", None),
            P(("section", "expert"), None),
            P(("section", "expert"), None),
            P(("section", "expert")),
            P(("section", "expert")),
        ),
        out_specs=(P(("section", "expert"), None), P(None, ("section", "expert")), P()),
        check_vma=False,
    )
```

```python
import math

import jax
import jax.numpy as jnp
from jax import lax
from jax.experimental import pallas as pl
from jax.experimental.pallas import tpu as pltpu
from jax.sharding import PartitionSpec as P

SOFTMAX_TEMPER = 0.05
AXES = ("section", "expert")
DOC_LEN = 2048
LANES = 128


def permutation(side, depth, axis_of_core, step):
    pairs = []
    for x in range(side):
        for y in range(side):
            for z in range(depth):
                for core in range(2):
                    to = ((x + step) % side, y) if axis_of_core[core] == 0 else (x, (y + step) % side)
                    here = ((x * side + y) * depth + z) * 2 + core
                    there = ((to[0] * side + to[1]) * depth + z) * 2 + core
                    pairs.append((here, there))
    return pairs


def z_permutation(side, depth, step):
    return [
        ((s * depth + z) * 2 + c, (s * depth + (z + step) % depth) * 2 + c)
        for s in range(side * side)
        for z in range(depth)
        for c in range(2)
    ]


def after(value, *earlier):
    return lax.optimization_barrier((value,) + earlier)[0]


NT = (((1,), (1,)), ((), ()))
TN = (((0,), (0,)), ((), ()))
WHOLE = pl.BlockSpec(memory_space=pltpu.VMEM)
IN_HBM = pl.BlockSpec(memory_space=pltpu.HBM)
QUICK = pl.CostEstimate(flops=1, bytes_accessed=1, transcendentals=0)


def params(mib):
    return pltpu.CompilerParams(vmem_limit_bytes=mib * 1024 * 1024)


def dot(a, b, dims=(((1,), (0,)), ((), ()))):
    return lax.dot_general(a, b, dims, preferred_element_type=jnp.float32)


def split(a):
    high = a.astype(jnp.bfloat16)
    return high, (a - high.astype(jnp.float32)).astype(jnp.bfloat16)


def place_kernel(experts, capacity, docs, tokens, routes, gates, doc, mask, filled, w_high, w_low, base):
    slots, count = w_high.shape
    features = tokens.shape[1]
    slot = lax.broadcasted_iota(jnp.int32, (slots, count), 0)
    expert = jnp.zeros((slots, count), jnp.int32)
    for e in range(1, experts):
        expert += (slot >= e * capacity).astype(jnp.int32)
    first = routes[0:1, :] == expert
    named = first | (routes[1:2, :] == expert)
    before = lax.broadcasted_iota(jnp.int32, (count, count), 0) < lax.broadcasted_iota(
        jnp.int32, (count, count), 1
    )
    one = jnp.float32(1)
    zero = jnp.float32(0)
    earlier = dot(
        jnp.where(named, one, zero).astype(jnp.bfloat16),
        jnp.where(before, one, zero).astype(jnp.bfloat16),
    )
    place = named & (earlier.astype(jnp.int32) == slot - expert * capacity)
    filled[:, :features] = dot(
        jnp.where(place, one, zero).astype(jnp.bfloat16), tokens[...]
    ).astype(jnp.bfloat16)
    weight = jnp.where(place, jnp.where(first, gates[0:1, :], gates[1:2, :]), zero)
    high, low = split(weight)
    w_high[...] = high
    w_low[...] = low
    lane_doc = lax.broadcasted_iota(jnp.int32, (LANES, count), 0)
    pooled = mask[...] == 1
    own = (doc[...] == lane_doc) & pooled & (lane_doc < docs)
    other = (doc[...] == lane_doc - docs) & pooled & (lane_doc < 2 * docs)
    own = jnp.where(own, one, zero)
    other = jnp.where(other, one, zero).astype(jnp.bfloat16)
    own_bf = own.astype(jnp.bfloat16)
    filled[:, features:] = (dot(high, own_bf, NT) + dot(low, other, NT)).astype(jnp.bfloat16)
    base[:, :features] = dot(own_bf[:docs], tokens[...])
    base[:, features:] = jnp.broadcast_to(
        jnp.sum(own[:docs], axis=1, keepdims=True), (docs, LANES)
    )


def place_tokens(tokens, routes, gates, doc, mask, experts, capacity, docs):
    count, features = tokens.shape
    slots = experts * capacity
    return pl.pallas_call(
        lambda *refs: place_kernel(experts, capacity, docs, *refs),
        out_specs=[WHOLE] * 4,
        out_shape=[
            jax.ShapeDtypeStruct((slots, features + LANES), jnp.bfloat16),
            jax.ShapeDtypeStruct((slots, count), jnp.bfloat16),
            jax.ShapeDtypeStruct((slots, count), jnp.bfloat16),
            jax.ShapeDtypeStruct((docs, features + LANES), jnp.float32),
        ],
        compiler_params=params(16),
        cost_estimate=QUICK,
    )(tokens, routes.T, gates.T, doc.reshape(1, count), mask.reshape(1, count))


def combine_kernel(tokens, w_high, w_low, returned, out):
    rows = returned[...]
    out[...] = (
        tokens[...].astype(jnp.float32) + dot(w_high[...], rows, TN) + dot(w_low[...], rows, TN)
    ).astype(jnp.bfloat16)


def combine(tokens, w_high, w_low, returned):
    return pl.pallas_call(
        combine_kernel,
        out_shape=jax.ShapeDtypeStruct(tokens.shape, jnp.bfloat16),
        compiler_params=params(16),
        cost_estimate=QUICK,
    )(tokens, w_high, w_low, returned)


def silu_times(gate, up):
    return (gate / (1.0 + jnp.exp(-gate)) * up).astype(jnp.bfloat16)


def experts_kernel(groups, pieces, plan, docs, *refs):
    x_count, w_count = sum(groups), sum(pieces)
    adds, keeps = plan
    sources, refs = refs[: x_count + w_count], refs[x_count + w_count :]
    if adds or keeps:
        acc_ref, refs = refs[0], refs[1:]
    out_ref, sums_ref, x_held, gates, ups, pooled, sem = refs[:7]
    downs = refs[7] if len(refs) > 7 else None
    step, steps = pl.program_id(0), pl.num_programs(0)
    _, width, features = gates.shape

    x_copies, at = [], 0
    for group, count in enumerate(groups):
        row, copies = 0, []
        for _ in range(count):
            rows = sources[at].shape[0]
            copies.append(
                pltpu.make_async_copy(
                    sources[at], x_held.at[group, row : row + rows, :], sem.at[at]
                )
            )
            row, at = row + rows, at + 1
        x_copies.append(copies)
    w_copies = []
    for piece, count in enumerate(pieces):
        copies = []
        for held in (gates, ups):
            copies.append(pltpu.make_async_copy(sources[at], held.at[piece], sem.at[at]))
            at += 1
        row = 0
        for _ in range(count - 2):
            rows = sources[at].shape[0]
            copies.append(
                pltpu.make_async_copy(
                    sources[at], downs.at[piece, row : row + rows, :], sem.at[at]
                )
            )
            row, at = row + rows, at + 1
        w_copies.append(copies)

    @pl.when(step == 0)
    def _():
        order = x_copies[0] + [c for cs in w_copies for c in cs] + [c for cs in x_copies[1:] for c in cs]
        for copy in order:
            copy.start()
        pooled[...] = jnp.zeros_like(pooled)

    for group in range(len(groups)):
        @pl.when(step == group)
        def _():
            for copy in x_copies[group]:
                copy.wait()

    def ready(copies):
        @pl.when(step == 0)
        def _():
            for copy in copies:
                copy.wait()

    x = x_held[step, :, :features]
    shares = x_held[step, :, features:]
    total = acc_ref[0] if adds else None
    for piece in range(len(pieces)):
        ready(w_copies[piece][:1])
        gate = dot(x, gates[piece], NT)
        ready(w_copies[piece][1:2])
        hidden = silu_times(gate, dot(x, ups[piece], NT))
        pooled[piece] += dot(shares, hidden, TN)
        if downs is None:
            out_ref[0, piece] = hidden
            continue
        ready(w_copies[piece][2:])
        out = dot(hidden, downs[piece])
        total = out if total is None else total + out
    if downs is not None:
        out_ref[0] = total

    @pl.when(step == steps - 1)
    def _():
        if downs is None:
            sums_ref[...] = pooled[...]
            return
        sums = jnp.zeros((docs, features), jnp.float32)
        for piece in range(len(pieces)):
            high, low = split(pooled[piece][:docs] + pooled[piece][docs : 2 * docs])
            sums += dot(high, downs[piece]) + dot(low, downs[piece])
        sums_ref[...] = sums


def run_experts(groups, pieces, docs, acc=None, first=0, total=None, adds=False):
    xs = [x for group in groups for x in group]
    weights = [w for piece in pieces for w in piece]
    block = sum(x.shape[0] for x in groups[0])
    wide = xs[0].shape[1]
    width, features = pieces[0][0].shape
    count = len(pieces)
    has_down = len(pieces[0]) > 2
    steps = len(groups)
    total = steps if total is None else total
    operands = xs + weights
    in_specs = [IN_HBM] * len(operands)
    aliases = {}
    if has_down:
        out_spec = pl.BlockSpec((1, block, features), lambda i: (i + first, 0, 0))
        out_shape = jax.ShapeDtypeStruct((total, block, features), jnp.float32)
        sums_shape = (docs, features)
        sums_spec = pl.BlockSpec(sums_shape, lambda i: (0, 0))
    else:
        out_spec = pl.BlockSpec((1, count, block, width), lambda i: (i + first, 0, 0, 0))
        out_shape = jax.ShapeDtypeStruct((total, count, block, width), jnp.bfloat16)
        sums_shape = (count, LANES, width)
        sums_spec = pl.BlockSpec(sums_shape, lambda i: (0, 0, 0))
    if acc is not None:
        in_specs.append(out_spec if adds else IN_HBM)
        operands.append(acc)
        aliases = {len(operands) - 1: 0}
    plan = (adds, acc is not None)
    scratch = [
        pltpu.VMEM((steps, block, wide), jnp.bfloat16),
        pltpu.VMEM((count, width, features), jnp.bfloat16),
        pltpu.VMEM((count, width, features), jnp.bfloat16),
        pltpu.VMEM((count, LANES, width), jnp.float32),
        pltpu.SemaphoreType.DMA((len(xs) + len(weights),)),
    ]
    if has_down:
        scratch.append(pltpu.VMEM((count, width, features), jnp.bfloat16))
    return pl.pallas_call(
        lambda *refs: experts_kernel(
            [len(g) for g in groups], [len(p) for p in pieces], plan, docs, *refs
        ),
        grid=(steps,),
        in_specs=in_specs,
        out_specs=[out_spec, sums_spec],
        out_shape=[out_shape, jax.ShapeDtypeStruct(sums_shape, jnp.float32)],
        scratch_shapes=scratch,
        input_output_aliases=aliases,
        compiler_params=params(40),
        cost_estimate=pl.CostEstimate(
            flops=(6 if has_down else 4) * steps * block * features * width * count,
            bytes_accessed=2 * sum(w.size for w in weights) + steps * block * features * 6,
            transcendentals=steps * block * width * count,
        ),
    )(*operands)


def add_downs_kernel(parts, docs, hidden, acc, pooled, *refs):
    downs, out, sums = refs[:-2], refs[-2], refs[-1]
    total = acc[0]
    pieces = hidden.shape[1]
    for piece in range(pieces):
        row = 0
        for down in downs[piece * parts : (piece + 1) * parts]:
            rows = down.shape[0]
            total += dot(hidden[0, piece, :, row : row + rows], down[...])
            row += rows
    out[0] = total

    @pl.when(pl.program_id(0) == pl.num_programs(0) - 1)
    def _():
        found = jnp.zeros(sums.shape, jnp.float32)
        for piece in range(pieces):
            high, low = split(pooled[piece][:docs] + pooled[piece][docs : 2 * docs])
            row = 0
            for down in downs[piece * parts : (piece + 1) * parts]:
                rows = down.shape[0]
                found += dot(high[:, row : row + rows], down[...])
                found += dot(low[:, row : row + rows], down[...])
                row += rows
        sums[...] = found


def add_downs(hidden, acc, pooled, pieces, docs):
    steps, count, block, width = hidden.shape
    features = acc.shape[2]
    downs = [d for piece in pieces for d in piece]
    by_block = pl.BlockSpec((1, block, features), lambda i: (i, 0, 0))
    once = pl.Buffered(1)
    return pl.pallas_call(
        lambda *refs: add_downs_kernel(len(pieces[0]), docs, *refs),
        grid=(steps,),
        in_specs=[
            pl.BlockSpec((1, count, block, width), lambda i: (i, 0, 0, 0)),
            by_block,
            pl.BlockSpec(pooled.shape, lambda i: (0, 0, 0), pipeline_mode=once),
        ]
        + [pl.BlockSpec(d.shape, lambda i: (0, 0), pipeline_mode=once) for d in downs],
        out_specs=[by_block, pl.BlockSpec((docs, features), lambda i: (0, 0))],
        out_shape=[
            jax.ShapeDtypeStruct(acc.shape, jnp.float32),
            jax.ShapeDtypeStruct((docs, features), jnp.float32),
        ],
        input_output_aliases={1: 0},
        compiler_params=params(32),
        cost_estimate=pl.CostEstimate(
            flops=2 * steps * block * features * width * count,
            bytes_accessed=2 * sum(d.size for d in downs) + steps * block * features * 10,
            transcendentals=0,
        ),
    )(hidden, acc, pooled, *downs)


def last_far_kernel(docs, hidden, acc, down, pooled, base, out_a, out_b, total):
    half, features = out_a.shape
    out = acc[0] + dot(hidden[0, 0], down[...])
    out_a[...] = out[:half].astype(jnp.bfloat16)
    out_b[...] = out[half:].astype(jnp.bfloat16)
    high, low = split(pooled[0, :docs] + pooled[0, docs : 2 * docs])
    total[:, :features] = base[:, :features] + dot(high, down[...]) + dot(low, down[...])
    total[:, features:] = base[:, features:]


def last_far(hidden, acc, down, pooled, base):
    _, count, features = acc.shape
    docs = base.shape[0]
    half = jax.ShapeDtypeStruct((count // 2, features), jnp.bfloat16)
    last = hidden.shape[0] - 1
    constant = lambda shape: pl.BlockSpec(shape, lambda i: (0,) * len(shape))
    return pl.pallas_call(
        lambda *refs: last_far_kernel(docs, *refs),
        grid=(1,),
        in_specs=[
            pl.BlockSpec((1,) + hidden.shape[1:], lambda i: (last, 0, 0, 0)),
            constant(acc.shape),
            constant(down.shape),
            constant(pooled.shape),
            constant(base.shape),
        ],
        out_specs=[constant(half.shape), constant(half.shape), constant(base.shape)],
        out_shape=[half, half, jax.ShapeDtypeStruct(base.shape, jnp.float32)],
        compiler_params=params(32),
        cost_estimate=QUICK,
    )(hidden, acc, down, pooled, base)


def last_near_kernel(hidden, acc, down, own, p_a, p_b, m_a, m_b):
    step = pl.program_id(0)
    half = p_a.shape[0]
    out = (acc[0] + dot(hidden[0, 0], down[...])).astype(jnp.bfloat16)

    @pl.when(step == 0)
    def _():
        p_a[...] = out[:half]
        p_b[...] = out[half:]

    @pl.when(step == 1)
    def _():
        m_a[...] = out[:half]
        m_b[...] = out[half:]

    @pl.when(step == 2)
    def _():
        own[...] = out


def last_near(hidden, acc, down):
    _, block, features = acc.shape
    shapes = [block] + [block // 2] * 4
    return pl.pallas_call(
        last_near_kernel,
        grid=(3,),
        in_specs=[
            pl.BlockSpec((1,) + hidden.shape[1:], lambda i: (lax.rem(i + 1, 3), 0, 0, 0)),
            pl.BlockSpec((1, block, features), lambda i: (lax.rem(i + 1, 3), 0, 0)),
            pl.BlockSpec(down.shape, lambda i: (0, 0), pipeline_mode=pl.Buffered(1)),
        ],
        out_specs=[
            pl.BlockSpec((n, features), lambda i: (0, 0), pipeline_mode=pl.Buffered(1))
            for n in shapes
        ],
        out_shape=[jax.ShapeDtypeStruct((n, features), jnp.bfloat16) for n in shapes],
        compiler_params=params(32),
        cost_estimate=QUICK,
    )(hidden, acc, down)


def finish_kernel(own, one, two, three, embeddings, loss):
    docs, features = embeddings.shape
    total = (own[...] + two[...]) + (one[...] + three[...])
    means = total[:, :features] / jnp.maximum(total[:, features : features + 1], 1.0)
    embeddings[...] = means
    products = lax.dot_general(
        means, means, NT, precision=lax.Precision.HIGHEST, preferred_element_type=jnp.float32
    )
    scale = lax.rsqrt(jnp.sum(means * means, axis=1, keepdims=True) / features + 1e-06)
    row = lax.broadcasted_iota(jnp.int32, (docs, docs), 0)
    column = lax.broadcasted_iota(jnp.int32, (docs, docs), 1)
    scale_of_column = jnp.sum(jnp.where(row == column, scale, 0.0), axis=0, keepdims=True)
    similarity = products * scale * scale_of_column / (features * SOFTMAX_TEMPER)
    odd = lax.rem(column, 2) == 1
    spread = jnp.sum(jnp.where(odd, jnp.exp(similarity), 0.0), axis=1, keepdims=True)
    matching = jnp.sum(jnp.where(column == row + 1, similarity, 0.0), axis=1, keepdims=True)
    even = lax.rem(lax.broadcasted_iota(jnp.int32, (docs, 1), 0), 2) == 0
    terms = jnp.where(even, jnp.log(spread) - matching, 0.0)
    loss[...] = jnp.sum(terms, axis=0, keepdims=True) / (docs // 2)


def finish(own, one, two, three, features):
    docs = own.shape[0]
    return pl.pallas_call(
        finish_kernel,
        out_specs=[WHOLE] * 2,
        out_shape=[
            jax.ShapeDtypeStruct((docs, features), jnp.float32),
            jax.ShapeDtypeStruct((1, 1), jnp.float32),
        ],
        compiler_params=params(16),
        cost_estimate=QUICK,
    )(own, one, two, three)


def shards(tokens, w_gate, w_up, w_down, routes, gates, document_index, pool_mask):
    tok_count, feature_total = tokens.shape
    choose = routes.shape[1]
    expert_count = lax.axis_size("expert")
    section_count = lax.axis_size("section")
    side = math.isqrt(section_count)
    depth = expert_count // 2
    capacity = tok_count * choose * 5 // (4 * expert_count)
    slots = expert_count * capacity
    device_count = section_count * expert_count
    doc_count = 2 * (tok_count * device_count // DOC_LEN)

    def by_weight(a, step):
        return lax.ppermute(a, AXES, permutation(side, depth, (0, 1), step))

    def by_token(a, step):
        return lax.ppermute(a, AXES, permutation(side, depth, (1, 0), step))

    gate, up, down = w_gate[0].T, w_up[0].T, w_down[0]
    gate_p, gate_m = by_weight(gate, 1), by_weight(gate, -1)
    up_p, up_m = by_weight(up, 1), by_weight(up, -1)

    filled, w_high, w_low, base = place_tokens(
        tokens, routes, gates, document_index, pool_mask, expert_count, capacity, doc_count
    )
    mine = lax.all_to_all(
        filled.reshape(expert_count, capacity, -1), "expert", split_axis=0, concat_axis=0, tiled=True
    ).reshape(slots, -1)
    mine = after(mine, gate_p, gate_m, up_p, up_m)
    token_p, token_m = by_token(mine, 1), by_token(mine, -1)

    run = lambda *args, **kwargs: run_experts(*args, doc_count, **kwargs)
    own_piece = (gate, up, down)
    near_pieces = [(gate_p, up_p), (gate_m, up_m)]
    acc, sums_0 = run([[mine]], [own_piece], total=3)
    hidden_2, pooled_20 = run([[after(mine, sums_0)]], near_pieces, total=3)
    down_late = after(down, pooled_20)
    down_p, down_m = by_weight(down_late, 1), by_weight(down_late, -1)
    token_p, token_m = lax.optimization_barrier((token_p, token_m, pooled_20))[:2]
    token_far = by_token(token_m, -1)
    acc, sums_1 = run([[token_p], [token_m]], [own_piece], acc=acc, first=1, total=3)
    hidden_2, pooled_21 = run(
        [[after(token_p, sums_1)], [token_m]], near_pieces, acc=hidden_2, first=1, total=3
    )
    pooled_2 = pooled_20 + pooled_21
    gate_far = by_weight(after(gate_p, pooled_21), 1)
    up_far = by_weight(after(up_m, pooled_21), -1)
    acc, sums_2 = add_downs(hidden_2, acc, pooled_2, [(down_p,), (down_m,)], doc_count)
    down_far = by_weight(after(down_p, sums_2), 1)
    far_rows = [after(token_far, sums_2)]
    acc_far, sums_3 = run(
        [far_rows], [own_piece, (gate_p, up_p, down_p), (gate_m, up_m, down_m)]
    )
    base = jnp.concatenate(
        [base[:, :feature_total] + sums_1 + sums_2 + sums_3 + sums_0, base[:, feature_total:]],
        axis=1,
    )

    far_piece = (after(gate_far, base), up_far)
    hidden_far, pooled_far = run([[mine], [token_p], [token_m], far_rows], [far_piece])
    out_far_a, out_far_b, total = last_far(hidden_far, acc_far, down_far, pooled_far, base)
    far_a, far_b = by_token(out_far_a, -1), by_token(out_far_b, 1)
    out_own, out_p_a, out_p_b, out_m_a, out_m_b = last_near(
        hidden_far, after(acc, total), down_far
    )

    from_m_b = by_token(out_p_b, -1)
    from_p_a = by_token(out_m_a, 1)
    relay_m = (out_p_a.astype(jnp.float32) + far_a.astype(jnp.float32)).astype(jnp.bfloat16)
    relay_p = (out_m_b.astype(jnp.float32) + far_b.astype(jnp.float32)).astype(jnp.bfloat16)
    from_m_a, from_p_b = by_token(relay_m, -1), by_token(relay_p, 1)
    expert_out = (
        out_own.astype(jnp.float32)
        + jnp.concatenate([from_m_a, from_m_b], axis=0).astype(jnp.float32)
        + jnp.concatenate([from_p_a, from_p_b], axis=0).astype(jnp.float32)
    ).astype(jnp.bfloat16)
    returned = lax.all_to_all(
        expert_out.reshape(expert_count, capacity, feature_total),
        "expert",
        split_axis=0,
        concat_axis=0,
        tiled=True,
    )
    moe_out = combine(tokens, w_high, w_low, returned.reshape(slots, feature_total))

    total = after(total, out_p_b)
    flip = [(i, i ^ 1) for i in range(device_count)]
    total = after(total + lax.ppermute(total, AXES, flip), relay_m, relay_p)
    pairs_z = lambda step: z_permutation(side, depth, step)
    pairs_t = lambda step: permutation(side, depth, (1, 0), step)
    pairs_w = lambda step: permutation(side, depth, (0, 1), step)
    for pairs_of in (pairs_z, pairs_t):
        one, two, three = (lax.ppermute(total, AXES, pairs_of(step)) for step in (1, 2, 3))
        total = (total + two) + (one + three)
    total = after(total, expert_out)
    one, two, three = (lax.ppermute(total, AXES, pairs_w(step)) for step in (1, 2, 3))
    embeddings, loss = finish(total, one, two, three, feature_total)
    share = feature_total // device_count
    emb_share = lax.dynamic_slice_in_dim(embeddings, lax.axis_index(AXES) * share, share, 1)
    return (moe_out, emb_share, loss[0, 0])


def solution(mesh):
    return jax.shard_map(
        shards,
        mesh=mesh,
        in_specs=(
            P(("section", "expert"), None),
            P("expert", None, "section"),
            P("expert", None, "section"),
            P("expert", "section", None),
            P(("section", "expert"), None),
            P(("section", "expert"), None),
            P(("section", "expert")),
            P(("section", "expert")),
        ),
        out_specs=(P(("section", "expert"), None), P(None, ("section", "expert")), P()),
        check_vma=False,
    )
```

```python
import math

import jax
import jax.numpy as jnp
from jax import lax
from jax.experimental import pallas as pl
from jax.experimental.pallas import tpu as pltpu
from jax.sharding import PartitionSpec as P

SOFTMAX_TEMPER = 0.05
AXES = ("section", "expert")
DOC_LEN = 2048
LANES = 128


def permutation(side, depth, axis_of_core, step):
    pairs = []
    for x in range(side):
        for y in range(side):
            for z in range(depth):
                for core in range(2):
                    to = ((x + step) % side, y) if axis_of_core[core] == 0 else (x, (y + step) % side)
                    here = ((x * side + y) * depth + z) * 2 + core
                    there = ((to[0] * side + to[1]) * depth + z) * 2 + core
                    pairs.append((here, there))
    return pairs


def z_permutation(side, depth, step):
    return [
        ((s * depth + z) * 2 + c, (s * depth + (z + step) % depth) * 2 + c)
        for s in range(side * side)
        for z in range(depth)
        for c in range(2)
    ]


def after(value, *earlier):
    return lax.optimization_barrier((value,) + earlier)[0]


NT = (((1,), (1,)), ((), ()))
TN = (((0,), (0,)), ((), ()))
WHOLE = pl.BlockSpec(memory_space=pltpu.VMEM)
SCRATCH = 14
QUICK = pl.CostEstimate(flops=1, bytes_accessed=1, transcendentals=0)


def params(mib):
    return pltpu.CompilerParams(vmem_limit_bytes=mib * 1024 * 1024)


def dot(a, b, dims=(((1,), (0,)), ((), ()))):
    return lax.dot_general(a, b, dims, preferred_element_type=jnp.float32)


def split(a):
    high = a.astype(jnp.bfloat16)
    return high, (a - high.astype(jnp.float32)).astype(jnp.bfloat16)


def place_kernel(experts, capacity, docs, tokens, routes, gates, doc, mask, filled, w_high, w_low, base):
    slots, count = w_high.shape
    features = tokens.shape[1]
    slot = lax.broadcasted_iota(jnp.int32, (slots, count), 0)
    expert = jnp.zeros((slots, count), jnp.int32)
    for e in range(1, experts):
        expert += (slot >= e * capacity).astype(jnp.int32)
    first = routes[0:1, :] == expert
    named = first | (routes[1:2, :] == expert)
    before = lax.broadcasted_iota(jnp.int32, (count, count), 0) < lax.broadcasted_iota(
        jnp.int32, (count, count), 1
    )
    one = jnp.float32(1)
    zero = jnp.float32(0)
    earlier = dot(
        jnp.where(named, one, zero).astype(jnp.bfloat16),
        jnp.where(before, one, zero).astype(jnp.bfloat16),
    )
    place = named & (earlier.astype(jnp.int32) == slot - expert * capacity)
    filled[:, :features] = dot(
        jnp.where(place, one, zero).astype(jnp.bfloat16), tokens[...]
    ).astype(jnp.bfloat16)
    weight = jnp.where(place, jnp.where(first, gates[0:1, :], gates[1:2, :]), zero)
    high, low = split(weight)
    w_high[...] = high
    w_low[...] = low
    lane_doc = lax.broadcasted_iota(jnp.int32, (LANES, count), 0)
    pooled = mask[...] == 1
    own = (doc[...] == lane_doc) & pooled & (lane_doc < docs)
    other = (doc[...] == lane_doc - docs) & pooled & (lane_doc < 2 * docs)
    own = jnp.where(own, one, zero)
    other = jnp.where(other, one, zero).astype(jnp.bfloat16)
    own_bf = own.astype(jnp.bfloat16)
    filled[:, features:] = (dot(high, own_bf, NT) + dot(low, other, NT)).astype(jnp.bfloat16)
    base[:, :features] = dot(own_bf[:docs], tokens[...])
    base[:, features:] = jnp.broadcast_to(
        jnp.sum(own[:docs], axis=1, keepdims=True), (docs, LANES)
    )


def place_tokens(tokens, routes, gates, doc, mask, experts, capacity, docs):
    count, features = tokens.shape
    slots = experts * capacity
    return pl.pallas_call(
        lambda *refs: place_kernel(experts, capacity, docs, *refs),
        out_specs=[WHOLE] * 4,
        out_shape=[
            jax.ShapeDtypeStruct((slots, features + LANES), jnp.bfloat16),
            jax.ShapeDtypeStruct((slots, count), jnp.bfloat16),
            jax.ShapeDtypeStruct((slots, count), jnp.bfloat16),
            jax.ShapeDtypeStruct((docs, features + LANES), jnp.float32),
        ],
        compiler_params=params(16),
        cost_estimate=QUICK,
    )(tokens, routes.T, gates.T, doc.reshape(1, count), mask.reshape(1, count))


def combine_kernel(tokens, w_high, w_low, returned, out):
    rows = returned[...]
    out[...] = (
        tokens[...].astype(jnp.float32) + dot(w_high[...], rows, TN) + dot(w_low[...], rows, TN)
    ).astype(jnp.bfloat16)


def combine(tokens, w_high, w_low, returned):
    return pl.pallas_call(
        combine_kernel,
        out_shape=jax.ShapeDtypeStruct(tokens.shape, jnp.bfloat16),
        compiler_params=params(16),
        cost_estimate=QUICK,
    )(tokens, w_high, w_low, returned)


def silu_times(gate, up):
    return (gate / (1.0 + jnp.exp(-gate)) * up).astype(jnp.bfloat16)


def experts_kernel(count, pieces, adds, docs, *refs):
    xs, refs = refs[:count], refs[count:]
    weights, refs = refs[: sum(pieces)], refs[sum(pieces) :]
    accs, refs = (refs[:count], refs[count:]) if adds else ([None] * count, refs)
    outs, sums_ref, pooled = refs[:-2], refs[-2], refs[-1]
    features = weights[0].shape[1]
    size = pieces[0]
    for group in range(count):
        x = xs[group][:, :features]
        shares = xs[group][:, features:]
        total = accs[group][...] if adds else None
        for piece in range(len(pieces)):
            gate, up = weights[size * piece], weights[size * piece + 1]
            hidden = silu_times(dot(x, gate[...], NT), dot(x, up[...], NT))
            found = dot(shares, hidden, TN)
            pooled[piece] = found if group == 0 else pooled[piece] + found
            if size == 2:
                outs[group * len(pieces) + piece][...] = hidden
                continue
            out = dot(hidden, weights[size * piece + 2][...])
            total = out if total is None else total + out
        if size > 2:
            outs[group][...] = total
    if size == 2:
        sums_ref[...] = pooled[...]
        return
    sums = jnp.zeros((docs, features), jnp.float32)
    for piece in range(len(pieces)):
        high, low = split(pooled[piece][:docs] + pooled[piece][docs : 2 * docs])
        down = weights[size * piece + 2][...]
        sums += dot(high, down) + dot(low, down)
    sums_ref[...] = sums


def run_experts(rows, pieces, docs, accs=None):
    weights = [w for piece in pieces for w in piece]
    block, wide = rows[0].shape
    width, features = weights[0].shape
    has_down = len(pieces[0]) > 2
    if has_down:
        out_shape = [jax.ShapeDtypeStruct((block, features), jnp.float32) for _ in rows]
        out_shape.append(jax.ShapeDtypeStruct((docs, features), jnp.float32))
    else:
        out_shape = [
            jax.ShapeDtypeStruct((block, width), jnp.bfloat16) for _ in rows for _ in pieces
        ]
        out_shape.append(jax.ShapeDtypeStruct((len(pieces), LANES, width), jnp.float32))
    operands = [*rows, *weights, *(accs or [])]
    work = len(rows) * block * features * width * len(pieces)
    *outs, sums = pl.pallas_call(
        lambda *refs: experts_kernel(
            len(rows), [len(p) for p in pieces], accs is not None, docs, *refs
        ),
        in_specs=[WHOLE] * len(operands),
        out_specs=[WHOLE] * len(out_shape),
        out_shape=out_shape,
        scratch_shapes=[pltpu.VMEM((len(pieces), LANES, width), jnp.float32)],
        compiler_params=params(SCRATCH),
        cost_estimate=pl.CostEstimate(
            flops=work,
            bytes_accessed=sum(w.size for w in weights) // 4,
            transcendentals=len(rows) * block * width * len(pieces),
        ),
    )(*operands)
    return outs, sums


def add_downs_kernel(groups, pieces, pooled_count, halves, docs, *refs):
    hidden, refs = refs[: groups * pieces], refs[groups * pieces :]
    accs, refs = refs[:groups], refs[groups:]
    downs, refs = refs[:pieces], refs[pieces:]
    pooled, refs = refs[:pooled_count], refs[pooled_count:]
    features = downs[0].shape[1]
    if pooled_count:
        base, refs = refs[0], refs[1:]
        outs, sums_ref = refs[:-1], refs[-1]
        sums = base[:, :features]
        for piece in range(pieces):
            both = pooled[0][piece]
            for other in pooled[1:]:
                both = both + other[piece]
            high, low = split(both[:docs] + both[docs : 2 * docs])
            sums += dot(high, downs[piece][...]) + dot(low, downs[piece][...])
        sums_ref[:, :features] = sums
        sums_ref[:, features:] = base[:, features:]
    else:
        outs = refs
    for group in range(groups):
        total = accs[group][...]
        for piece in range(pieces):
            total += dot(hidden[group * pieces + piece][...], downs[piece][...])
        if halves:
            half = total.shape[0] // 2
            outs[2 * group][...] = total[:half].astype(jnp.bfloat16)
            outs[2 * group + 1][...] = total[half:].astype(jnp.bfloat16)
        else:
            outs[group][...] = total.astype(outs[group].dtype)


def add_downs(hidden, accs, downs, docs, pooled=(), base=None, halves=False, dtype=jnp.bfloat16):
    block, features = accs[0].shape
    width = hidden[0][0].shape[1]
    if halves:
        out_shape = [
            jax.ShapeDtypeStruct((block // 2, features), dtype) for _ in range(2 * len(accs))
        ]
    else:
        out_shape = [jax.ShapeDtypeStruct((block, features), dtype) for _ in accs]
    operands = [h for group in hidden for h in group] + [*accs, *downs, *pooled]
    if pooled:
        operands.append(base)
        out_shape.append(jax.ShapeDtypeStruct(base.shape, jnp.float32))
    return pl.pallas_call(
        lambda *refs: add_downs_kernel(len(accs), len(downs), len(pooled), halves, docs, *refs),
        in_specs=[WHOLE] * len(operands),
        out_specs=[WHOLE] * len(out_shape),
        out_shape=out_shape,
        compiler_params=params(SCRATCH),
        cost_estimate=pl.CostEstimate(
            flops=len(accs) * block * features * width * len(downs) // 2,
            bytes_accessed=sum(d.size for d in downs) // 4,
            transcendentals=0,
        ),
    )(*operands)


def finish_kernel(own, one, two, three, embeddings, loss):
    docs, features = embeddings.shape
    total = (own[...] + two[...]) + (one[...] + three[...])
    means = total[:, :features] / jnp.maximum(total[:, features : features + 1], 1.0)
    embeddings[...] = means
    products = lax.dot_general(
        means, means, NT, precision=lax.Precision.HIGHEST, preferred_element_type=jnp.float32
    )
    scale = lax.rsqrt(jnp.sum(means * means, axis=1, keepdims=True) / features + 1e-06)
    row = lax.broadcasted_iota(jnp.int32, (docs, docs), 0)
    column = lax.broadcasted_iota(jnp.int32, (docs, docs), 1)
    scale_of_column = jnp.sum(jnp.where(row == column, scale, 0.0), axis=0, keepdims=True)
    similarity = products * scale * scale_of_column / (features * SOFTMAX_TEMPER)
    odd = lax.rem(column, 2) == 1
    spread = jnp.sum(jnp.where(odd, jnp.exp(similarity), 0.0), axis=1, keepdims=True)
    matching = jnp.sum(jnp.where(column == row + 1, similarity, 0.0), axis=1, keepdims=True)
    even = lax.rem(lax.broadcasted_iota(jnp.int32, (docs, 1), 0), 2) == 0
    terms = jnp.where(even, jnp.log(spread) - matching, 0.0)
    loss[...] = jnp.sum(terms, axis=0, keepdims=True) / (docs // 2)


def finish(own, one, two, three, features):
    docs = own.shape[0]
    return pl.pallas_call(
        finish_kernel,
        out_specs=[WHOLE] * 2,
        out_shape=[
            jax.ShapeDtypeStruct((docs, features), jnp.float32),
            jax.ShapeDtypeStruct((1, 1), jnp.float32),
        ],
        compiler_params=params(16),
        cost_estimate=QUICK,
    )(own, one, two, three)


def shards(tokens, w_gate, w_up, w_down, routes, gates, document_index, pool_mask):
    tok_count, feature_total = tokens.shape
    choose = routes.shape[1]
    expert_count = lax.axis_size("expert")
    section_count = lax.axis_size("section")
    side = math.isqrt(section_count)
    depth = expert_count // 2
    capacity = tok_count * choose * 5 // (4 * expert_count)
    slots = expert_count * capacity
    device_count = section_count * expert_count
    doc_count = 2 * (tok_count * device_count // DOC_LEN)

    def by_weight(a, step):
        return lax.ppermute(a, AXES, permutation(side, depth, (0, 1), step))

    def by_token(a, step):
        return lax.ppermute(a, AXES, permutation(side, depth, (1, 0), step))

    gate, up, down = w_gate[0].T, w_up[0].T, w_down[0]
    gate_p, gate_m = by_weight(gate, 1), by_weight(gate, -1)
    up_p, up_m = by_weight(up, 1), by_weight(up, -1)

    filled, w_high, w_low, base = place_tokens(
        tokens, routes, gates, document_index, pool_mask, expert_count, capacity, doc_count
    )
    mine = lax.all_to_all(
        filled.reshape(expert_count, capacity, -1), "expert", split_axis=0, concat_axis=0, tiled=True
    ).reshape(slots, -1)
    token_p, token_m = by_token(mine, 1), by_token(mine, -1)

    docs = doc_count
    own_piece = (gate, up, down)
    near_pieces = [(gate_p, up_p), (gate_m, up_m)]
    mine = after(mine, gate_p, gate_m, up_p, up_m)
    (acc_mine,), sums_0 = run_experts([mine], [own_piece], docs)
    hidden_mine, pooled_0 = run_experts([after(mine, sums_0)], near_pieces, docs)
    down_late = after(down, gate_p, gate_m, up_p, up_m)
    down_p, down_m = by_weight(down_late, 1), by_weight(down_late, -1)
    token_p, token_m = lax.optimization_barrier((token_p, token_m, pooled_0))[:2]
    token_far = by_token(token_m, -1)
    (acc_p, acc_m), sums_1 = run_experts([token_p, token_m], [own_piece], docs)
    (h_pp, h_pm, h_mp, h_mm), pooled_1 = run_experts(
        [after(token_p, sums_1), token_m], near_pieces, docs
    )
    gate_far = by_weight(after(gate_p, pooled_0), 1)
    up_far = by_weight(after(up_m, pooled_0), -1)
    acc_p, acc_m, base = add_downs(
        [[h_pp, h_pm], [h_mp, h_mm]],
        [acc_p, acc_m],
        [down_p, down_m],
        docs,
        pooled=[pooled_0, pooled_1],
        base=base,
        dtype=jnp.float32,
    )
    down_far = by_weight(after(down_p, pooled_1), 1)
    token_far = after(token_far, base)
    (acc_far,), sums_2 = run_experts(
        [token_far], [own_piece, (gate_p, up_p, down_p), (gate_m, up_m, down_m)], docs
    )
    base = jnp.concatenate(
        [base[:, :feature_total] + sums_0 + sums_1 + sums_2, base[:, feature_total:]], axis=1
    )

    far_piece = (after(gate_far, base), up_far)
    (h_far, h_p, h_m, h_mine), pooled_2 = run_experts(
        [token_far, token_p, token_m, mine], [far_piece], docs
    )
    out_far_a, out_far_b, total = add_downs(
        [[h_far]], [acc_far], [down_far], docs, pooled=[pooled_2], base=base, halves=True
    )
    far_a, far_b = by_token(out_far_a, -1), by_token(out_far_b, 1)
    out_p_a, out_p_b, out_m_a, out_m_b = add_downs(
        [[h_p], [h_m]], [after(acc_p, total), acc_m], [down_far], docs, halves=True
    )
    (out_own,) = add_downs(
        [[*hidden_mine, h_mine]], [after(acc_mine, out_m_b)], [down_p, down_m, down_far], docs
    )

    from_m_b = by_token(out_p_b, -1)
    from_p_a = by_token(out_m_a, 1)
    relay_m = (out_p_a.astype(jnp.float32) + far_a.astype(jnp.float32)).astype(jnp.bfloat16)
    relay_p = (out_m_b.astype(jnp.float32) + far_b.astype(jnp.float32)).astype(jnp.bfloat16)
    from_m_a, from_p_b = by_token(relay_m, -1), by_token(relay_p, 1)
    expert_out = (
        out_own.astype(jnp.float32)
        + jnp.concatenate([from_m_a, from_m_b], axis=0).astype(jnp.float32)
        + jnp.concatenate([from_p_a, from_p_b], axis=0).astype(jnp.float32)
    ).astype(jnp.bfloat16)
    returned = lax.all_to_all(
        expert_out.reshape(expert_count, capacity, feature_total),
        "expert",
        split_axis=0,
        concat_axis=0,
        tiled=True,
    )
    moe_out = combine(tokens, w_high, w_low, returned.reshape(slots, feature_total))

    flip = [(i, i ^ 1) for i in range(device_count)]
    total = after(total + lax.ppermute(total, AXES, flip), relay_m, relay_p)
    pairs_z = lambda step: z_permutation(side, depth, step)
    pairs_t = lambda step: permutation(side, depth, (1, 0), step)
    pairs_w = lambda step: permutation(side, depth, (0, 1), step)
    for pairs_of in (pairs_z, pairs_t):
        one, two, three = (lax.ppermute(total, AXES, pairs_of(step)) for step in (1, 2, 3))
        total = (total + two) + (one + three)
    total = after(total, expert_out)
    one, two, three = (lax.ppermute(total, AXES, pairs_w(step)) for step in (1, 2, 3))
    embeddings, loss = finish(total, one, two, three, feature_total)
    share = feature_total // device_count
    emb_share = lax.dynamic_slice_in_dim(embeddings, lax.axis_index(AXES) * share, share, 1)
    return (moe_out, emb_share, loss[0, 0])


def solution(mesh):
    return jax.shard_map(
        shards,
        mesh=mesh,
        in_specs=(
            P(("section", "expert"), None),
            P("expert", None, "section"),
            P("expert", None, "section"),
            P("expert", "section", None),
            P(("section", "expert"), None),
            P(("section", "expert"), None),
            P(("section", "expert")),
            P(("section", "expert")),
        ),
        out_specs=(P(("section", "expert"), None), P(None, ("section", "expert")), P()),
        check_vma=False,
    )
```

```python
import math

import jax
import jax.numpy as jnp
from jax import lax
from jax.experimental import pallas as pl
from jax.experimental.pallas import tpu as pltpu
from jax.sharding import PartitionSpec as P

SOFTMAX_TEMPER = 0.05
AXES = ("section", "expert")
DOC_LEN = 2048
LANES = 128


def permutation(side, depth, axis_of_core, step):
    pairs = []
    for x in range(side):
        for y in range(side):
            for z in range(depth):
                for core in range(2):
                    to = ((x + step) % side, y) if axis_of_core[core] == 0 else (x, (y + step) % side)
                    here = ((x * side + y) * depth + z) * 2 + core
                    there = ((to[0] * side + to[1]) * depth + z) * 2 + core
                    pairs.append((here, there))
    return pairs


def z_permutation(side, depth, step):
    return [
        ((s * depth + z) * 2 + c, (s * depth + (z + step) % depth) * 2 + c)
        for s in range(side * side)
        for z in range(depth)
        for c in range(2)
    ]


def after(value, *earlier):
    return lax.optimization_barrier((value,) + earlier)[0]


NT = (((1,), (1,)), ((), ()))
TN = (((0,), (0,)), ((), ()))
WHOLE = pl.BlockSpec(memory_space=pltpu.VMEM)
SCRATCH = 14
QUICK = pl.CostEstimate(flops=1, bytes_accessed=1, transcendentals=0)


def params(mib):
    return pltpu.CompilerParams(vmem_limit_bytes=mib * 1024 * 1024)


def dot(a, b, dims=(((1,), (0,)), ((), ()))):
    return lax.dot_general(a, b, dims, preferred_element_type=jnp.float32)


def split(a):
    high = a.astype(jnp.bfloat16)
    return high, (a - high.astype(jnp.float32)).astype(jnp.bfloat16)


def place_kernel(experts, capacity, docs, tokens, routes, gates, doc, mask, filled, w_high, w_low, base):
    slots, count = w_high.shape
    features = tokens.shape[1]
    slot = lax.broadcasted_iota(jnp.int32, (slots, count), 0)
    expert = jnp.zeros((slots, count), jnp.int32)
    for e in range(1, experts):
        expert += (slot >= e * capacity).astype(jnp.int32)
    first = routes[0:1, :] == expert
    named = first | (routes[1:2, :] == expert)
    before = lax.broadcasted_iota(jnp.int32, (count, count), 0) < lax.broadcasted_iota(
        jnp.int32, (count, count), 1
    )
    one = jnp.float32(1)
    zero = jnp.float32(0)
    earlier = dot(
        jnp.where(named, one, zero).astype(jnp.bfloat16),
        jnp.where(before, one, zero).astype(jnp.bfloat16),
    )
    place = named & (earlier.astype(jnp.int32) == slot - expert * capacity)
    filled[:, :features] = dot(
        jnp.where(place, one, zero).astype(jnp.bfloat16), tokens[...]
    ).astype(jnp.bfloat16)
    weight = jnp.where(place, jnp.where(first, gates[0:1, :], gates[1:2, :]), zero)
    high, low = split(weight)
    w_high[...] = high
    w_low[...] = low
    lane_doc = lax.broadcasted_iota(jnp.int32, (LANES, count), 0)
    pooled = mask[...] == 1
    own = (doc[...] == lane_doc) & pooled & (lane_doc < docs)
    other = (doc[...] == lane_doc - docs) & pooled & (lane_doc < 2 * docs)
    own = jnp.where(own, one, zero)
    other = jnp.where(other, one, zero).astype(jnp.bfloat16)
    own_bf = own.astype(jnp.bfloat16)
    filled[:, features:] = (dot(high, own_bf, NT) + dot(low, other, NT)).astype(jnp.bfloat16)
    base[:, :features] = dot(own_bf[:docs], tokens[...])
    base[:, features:] = jnp.broadcast_to(
        jnp.sum(own[:docs], axis=1, keepdims=True), (docs, LANES)
    )


def place_tokens(tokens, routes, gates, doc, mask, experts, capacity, docs):
    count, features = tokens.shape
    slots = experts * capacity
    return pl.pallas_call(
        lambda *refs: place_kernel(experts, capacity, docs, *refs),
        out_specs=[WHOLE] * 4,
        out_shape=[
            jax.ShapeDtypeStruct((slots, features + LANES), jnp.bfloat16),
            jax.ShapeDtypeStruct((slots, count), jnp.bfloat16),
            jax.ShapeDtypeStruct((slots, count), jnp.bfloat16),
            jax.ShapeDtypeStruct((docs, features + LANES), jnp.float32),
        ],
        compiler_params=params(16),
        cost_estimate=QUICK,
    )(tokens, routes.T, gates.T, doc.reshape(1, count), mask.reshape(1, count))


def combine_kernel(tokens, w_high, w_low, returned, out):
    rows = returned[...]
    out[...] = (
        tokens[...].astype(jnp.float32) + dot(w_high[...], rows, TN) + dot(w_low[...], rows, TN)
    ).astype(jnp.bfloat16)


def combine(tokens, w_high, w_low, returned):
    return pl.pallas_call(
        combine_kernel,
        out_shape=jax.ShapeDtypeStruct(tokens.shape, jnp.bfloat16),
        compiler_params=params(16),
        cost_estimate=QUICK,
    )(tokens, w_high, w_low, returned)


def silu_times(gate, up):
    return (gate / (1.0 + jnp.exp(-gate)) * up).astype(jnp.bfloat16)


def experts_kernel(parts, pieces, adds, docs, *refs):
    xs = []
    for part in parts:
        xs.append(refs[:part])
        refs = refs[part:]
    count = len(parts)
    weights, refs = refs[: sum(pieces)], refs[sum(pieces) :]
    accs, refs = (refs[:count], refs[count:]) if adds else ([None] * count, refs)
    outs, sums_ref, pooled = refs[:-2], refs[-2], refs[-1]
    features = weights[0].shape[1]
    size = pieces[0]
    for group in range(count):
        x = jnp.concatenate([part[:, :features] for part in xs[group]], axis=0)
        shares = jnp.concatenate([part[:, features:] for part in xs[group]], axis=0)
        total = accs[group][...] if adds else None
        for piece in range(len(pieces)):
            gate, up = weights[size * piece], weights[size * piece + 1]
            hidden = silu_times(dot(x, gate[...], NT), dot(x, up[...], NT))
            found = dot(shares, hidden, TN)
            pooled[piece] = found if group == 0 else pooled[piece] + found
            if size == 2:
                outs[group * len(pieces) + piece][...] = hidden
                continue
            out = dot(hidden, weights[size * piece + 2][...])
            total = out if total is None else total + out
        if size > 2:
            outs[group][...] = total
    if size == 2:
        sums_ref[...] = pooled[...]
        return
    sums = jnp.zeros((docs, features), jnp.float32)
    for piece in range(len(pieces)):
        high, low = split(pooled[piece][:docs] + pooled[piece][docs : 2 * docs])
        down = weights[size * piece + 2][...]
        sums += dot(high, down) + dot(low, down)
    sums_ref[...] = sums


def run_experts(rows, pieces, docs, accs=None):
    weights = [w for piece in pieces for w in piece]
    block = sum(part.shape[0] for part in rows[0])
    width, features = weights[0].shape
    has_down = len(pieces[0]) > 2
    if has_down:
        out_shape = [jax.ShapeDtypeStruct((block, features), jnp.float32) for _ in rows]
        out_shape.append(jax.ShapeDtypeStruct((docs, features), jnp.float32))
    else:
        out_shape = [
            jax.ShapeDtypeStruct((block, width), jnp.bfloat16) for _ in rows for _ in pieces
        ]
        out_shape.append(jax.ShapeDtypeStruct((len(pieces), LANES, width), jnp.float32))
    operands = [part for group in rows for part in group] + [*weights, *(accs or [])]
    work = len(rows) * block * features * width * len(pieces)
    *outs, sums = pl.pallas_call(
        lambda *refs: experts_kernel(
            [len(r) for r in rows], [len(p) for p in pieces], accs is not None, docs, *refs
        ),
        in_specs=[WHOLE] * len(operands),
        out_specs=[WHOLE] * len(out_shape),
        out_shape=out_shape,
        scratch_shapes=[pltpu.VMEM((len(pieces), LANES, width), jnp.float32)],
        compiler_params=params(SCRATCH),
        cost_estimate=pl.CostEstimate(
            flops=work,
            bytes_accessed=sum(w.size for w in weights) // 4,
            transcendentals=len(rows) * block * width * len(pieces),
        ),
    )(*operands)
    return outs, sums


def add_downs_kernel(groups, pieces_parts, pooled_count, halves, docs, *refs):
    pieces = len(pieces_parts)
    hidden, refs = refs[: groups * pieces], refs[groups * pieces :]
    accs, refs = refs[:groups], refs[groups:]
    downs = []
    for parts in pieces_parts:
        downs.append(refs[:parts])
        refs = refs[parts:]
    pooled, refs = refs[:pooled_count], refs[pooled_count:]
    features = accs[0].shape[1]

    def product(a, piece):
        return jnp.concatenate([dot(a, part[...]) for part in downs[piece]], axis=1)

    if pooled_count:
        base, refs = refs[0], refs[1:]
        outs, sums_ref = refs[:-1], refs[-1]
        sums = base[:, :features]
        for piece in range(pieces):
            both = pooled[0][piece]
            for other in pooled[1:]:
                both = both + other[piece]
            high, low = split(both[:docs] + both[docs : 2 * docs])
            sums += product(high, piece) + product(low, piece)
        sums_ref[:, :features] = sums
        sums_ref[:, features:] = base[:, features:]
    else:
        outs = refs
    for group in range(groups):
        total = accs[group][...]
        for piece in range(pieces):
            total += product(hidden[group * pieces + piece][...], piece)
        if halves:
            half = total.shape[0] // 2
            outs[2 * group][...] = total[:half].astype(jnp.bfloat16)
            outs[2 * group + 1][...] = total[half:].astype(jnp.bfloat16)
        else:
            outs[group][...] = total.astype(outs[group].dtype)


def add_downs(hidden, accs, downs, docs, pooled=(), base=None, halves=False, dtype=jnp.bfloat16):
    block, features = accs[0].shape
    width = hidden[0][0].shape[1]
    if halves:
        out_shape = [
            jax.ShapeDtypeStruct((block // 2, features), dtype) for _ in range(2 * len(accs))
        ]
    else:
        out_shape = [jax.ShapeDtypeStruct((block, features), dtype) for _ in accs]
    operands = [h for group in hidden for h in group] + [*accs, *[part for down in downs for part in down], *pooled]
    if pooled:
        operands.append(base)
        out_shape.append(jax.ShapeDtypeStruct(base.shape, jnp.float32))
    return pl.pallas_call(
        lambda *refs: add_downs_kernel(
            len(accs), [len(down) for down in downs], len(pooled), halves, docs, *refs
        ),
        in_specs=[WHOLE] * len(operands),
        out_specs=[WHOLE] * len(out_shape),
        out_shape=out_shape,
        compiler_params=params(SCRATCH),
        cost_estimate=pl.CostEstimate(
            flops=len(accs) * block * features * width * len(downs) // 2,
            bytes_accessed=len(downs) * width * features // 4,
            transcendentals=0,
        ),
    )(*operands)


def add_parts_kernel(own, m_a, m_b, p_a, p_b, out):
    half = m_a.shape[0]
    for at, m, p in ((0, m_a, p_a), (half, m_b, p_b)):
        out[at : at + half, :] = (
            own[at : at + half, :].astype(jnp.float32)
            + m[...].astype(jnp.float32)
            + p[...].astype(jnp.float32)
        ).astype(jnp.bfloat16)


def add_parts(own, m_a, m_b, p_a, p_b):
    return pl.pallas_call(
        add_parts_kernel,
        in_specs=[WHOLE] * 5,
        out_specs=WHOLE,
        out_shape=jax.ShapeDtypeStruct(own.shape, jnp.bfloat16),
        compiler_params=params(SCRATCH),
        cost_estimate=QUICK,
    )(own, m_a, m_b, p_a, p_b)


def finish_kernel(features, first, own, one, two, three, part, loss):
    docs, share = part.shape
    total = (own[...] + two[...]) + (one[...] + three[...])
    means = total[:, :features] / jnp.maximum(total[:, features : features + 1], 1.0)
    part[...] = pltpu.roll(means, features - first[0], 1)[:, :share]
    products = lax.dot_general(
        means, means, NT, precision=lax.Precision.HIGHEST, preferred_element_type=jnp.float32
    )
    scale = lax.rsqrt(jnp.sum(means * means, axis=1, keepdims=True) / features + 1e-06)
    row = lax.broadcasted_iota(jnp.int32, (docs, docs), 0)
    column = lax.broadcasted_iota(jnp.int32, (docs, docs), 1)
    scale_of_column = jnp.sum(jnp.where(row == column, scale, 0.0), axis=0, keepdims=True)
    similarity = products * scale * scale_of_column / (features * SOFTMAX_TEMPER)
    odd = lax.rem(column, 2) == 1
    spread = jnp.sum(jnp.where(odd, jnp.exp(similarity), 0.0), axis=1, keepdims=True)
    matching = jnp.sum(jnp.where(column == row + 1, similarity, 0.0), axis=1, keepdims=True)
    even = lax.rem(lax.broadcasted_iota(jnp.int32, (docs, 1), 0), 2) == 0
    terms = jnp.where(even, jnp.log(spread) - matching, 0.0)
    loss[...] = jnp.sum(terms, axis=0, keepdims=True) / (docs // 2)


def finish(own, one, two, three, features, first, share):
    docs = own.shape[0]
    return pl.pallas_call(
        lambda *refs: finish_kernel(features, *refs),
        in_specs=[pl.BlockSpec(memory_space=pltpu.SMEM)] + [WHOLE] * 4,
        out_specs=[WHOLE] * 2,
        out_shape=[
            jax.ShapeDtypeStruct((docs, share), jnp.float32),
            jax.ShapeDtypeStruct((1, 1), jnp.float32),
        ],
        compiler_params=params(16),
        cost_estimate=QUICK,
    )(first, own, one, two, three)


def shards(tokens, w_gate, w_up, w_down, routes, gates, document_index, pool_mask):
    tok_count, feature_total = tokens.shape
    choose = routes.shape[1]
    expert_count = lax.axis_size("expert")
    section_count = lax.axis_size("section")
    side = math.isqrt(section_count)
    depth = expert_count // 2
    capacity = tok_count * choose * 5 // (4 * expert_count)
    slots = expert_count * capacity
    half_slots, half_features = slots // 2, feature_total // 2
    device_count = section_count * expert_count
    doc_count = 2 * (tok_count * device_count // DOC_LEN)

    def by_weight(a, step):
        return lax.ppermute(a, AXES, permutation(side, depth, (0, 1), step))

    def by_token(a, step):
        return lax.ppermute(a, AXES, permutation(side, depth, (1, 0), step))

    gate, up, down = w_gate[0].T, w_up[0].T, w_down[0]
    gate_p, gate_m = by_weight(gate, 1), by_weight(gate, -1)
    up_p, up_m = by_weight(up, 1), by_weight(up, -1)

    filled, w_high, w_low, base = place_tokens(
        tokens, routes, gates, document_index, pool_mask, expert_count, capacity, doc_count
    )
    mine = lax.all_to_all(
        filled.reshape(expert_count, capacity, -1), "expert", split_axis=0, concat_axis=0, tiled=True
    ).reshape(slots, -1)
    token_p, token_m = by_token(mine, 1), by_token(mine, -1)

    docs = doc_count
    own_piece = (gate, up, down)
    near_pieces = [(gate_p, up_p), (gate_m, up_m)]
    mine = after(mine, gate_p, gate_m, up_p, up_m)
    (acc_mine,), sums_0 = run_experts([(mine,)], [own_piece], docs)
    hidden_mine, pooled_0 = run_experts([(after(mine, sums_0),)], near_pieces, docs)
    down_late = after(down, gate_p, gate_m, up_p, up_m)
    down_p, down_m = by_weight(down_late, 1), by_weight(down_late, -1)
    token_p, token_m = lax.optimization_barrier((token_p, token_m, pooled_0))[:2]
    token_far = by_token(token_m, -1)
    (acc_p, acc_m), sums_1 = run_experts([(token_p,), (token_m,)], [own_piece], docs)
    (h_pp, h_pm, h_mp, h_mm), pooled_1 = run_experts(
        [(after(token_p, sums_1),), (token_m,)], near_pieces, docs
    )
    gate_far = by_weight(after(gate_p, pooled_0), 1)
    up_far = by_weight(after(up_m, pooled_0), -1)
    acc_p, acc_m, base = add_downs(
        [[h_pp, h_pm], [h_mp, h_mm]],
        [acc_p, acc_m],
        [(down_p,), (down_m,)],
        docs,
        pooled=[pooled_0, pooled_1],
        base=base,
        dtype=jnp.float32,
    )
    down_far = (by_weight(after(down_p, pooled_1), 1),)
    token_far = (after(token_far, base),)
    (acc_far,), sums_2 = run_experts(
        [token_far], [own_piece, (gate_p, up_p, down_p), (gate_m, up_m, down_m)], docs
    )
    base = jnp.concatenate(
        [base[:, :feature_total] + sums_0 + sums_1 + sums_2, base[:, feature_total:]], axis=1
    )

    far_piece = (after(gate_far, base), up_far)
    (h_far,), pooled_2 = run_experts([token_far], [far_piece], docs)
    out_far_a, out_far_b = add_downs([[h_far]], [acc_far], [down_far], docs, halves=True)
    far_a, far_b = by_token(out_far_a, -1), by_token(out_far_b, 1)
    (h_p, h_m), pooled_3 = run_experts(
        [(after(token_p, out_far_b),), (token_m,)], [far_piece], docs
    )
    out_p_a, out_p_b, out_m_a, out_m_b = add_downs(
        [[h_p], [h_m]], [acc_p, acc_m], [down_far], docs, halves=True
    )

    from_m_b = by_token(out_p_b, -1)
    from_p_a = by_token(out_m_a, 1)
    relay_m = (out_p_a.astype(jnp.float32) + far_a.astype(jnp.float32)).astype(jnp.bfloat16)
    relay_p = (out_m_b.astype(jnp.float32) + far_b.astype(jnp.float32)).astype(jnp.bfloat16)
    from_m_a, from_p_b = by_token(relay_m, -1), by_token(relay_p, 1)
    (h_mine,), pooled_4 = run_experts([(after(mine, relay_m, relay_p),)], [far_piece], docs)
    acc_mine, total = add_downs(
        [[h_mine]],
        [acc_mine],
        [down_far],
        docs,
        pooled=[pooled_2, pooled_3, pooled_4],
        base=base,
        dtype=jnp.float32,
    )
    (out_own,) = add_downs(
        [hidden_mine], [after(acc_mine, total)], [(down_p,), (down_m,)], docs
    )
    expert_out = add_parts(out_own, from_m_a, from_m_b, from_p_a, from_p_b)
    returned = lax.all_to_all(
        expert_out.reshape(expert_count, capacity, feature_total),
        "expert",
        split_axis=0,
        concat_axis=0,
        tiled=True,
    )
    moe_out = combine(tokens, w_high, w_low, returned.reshape(slots, feature_total))

    flip = [(i, i ^ 1) for i in range(device_count)]
    total = total + lax.ppermute(total, AXES, flip)
    pairs_z = lambda step: z_permutation(side, depth, step)
    pairs_t = lambda step: permutation(side, depth, (1, 0), step)
    pairs_w = lambda step: permutation(side, depth, (0, 1), step)
    for pairs_of in (pairs_z, pairs_t):
        one, two, three = (lax.ppermute(total, AXES, pairs_of(step)) for step in (1, 2, 3))
        total = (total + two) + (one + three)
    total = after(total, expert_out)
    one, two, three = (lax.ppermute(total, AXES, pairs_w(step)) for step in (1, 2, 3))
    share = feature_total // device_count
    first = (lax.axis_index(AXES) * share).astype(jnp.int32).reshape(1)
    emb_share, loss = finish(total, one, two, three, feature_total, first, share)
    return (moe_out, emb_share, loss[0, 0])


def solution(mesh):
    return jax.shard_map(
        shards,
        mesh=mesh,
        in_specs=(
            P(("section", "expert"), None),
            P("expert", None, "section"),
            P("expert", None, "section"),
            P("expert", "section", None),
            P(("section", "expert"), None),
            P(("section", "expert"), None),
            P(("section", "expert")),
            P(("section", "expert")),
        ),
        out_specs=(P(("section", "expert"), None), P(None, ("section", "expert")), P()),
        check_vma=False,
    )
```

```python
import math

import jax
import jax.numpy as jnp
from jax import lax
from jax.experimental import pallas as pl
from jax.experimental.pallas import tpu as pltpu
from jax.sharding import PartitionSpec as P

SOFTMAX_TEMPER = 0.05
AXES = ("section", "expert")
DOC_LEN = 2048
LANES = 128


def permutation(side, depth, axis_of_core, step):
    pairs = []
    for x in range(side):
        for y in range(side):
            for z in range(depth):
                for core in range(2):
                    to = ((x + step) % side, y) if axis_of_core[core] == 0 else (x, (y + step) % side)
                    here = ((x * side + y) * depth + z) * 2 + core
                    there = ((to[0] * side + to[1]) * depth + z) * 2 + core
                    pairs.append((here, there))
    return pairs


def z_permutation(side, depth, step):
    return [
        ((s * depth + z) * 2 + c, (s * depth + (z + step) % depth) * 2 + c)
        for s in range(side * side)
        for z in range(depth)
        for c in range(2)
    ]


def after(value, *earlier):
    return lax.optimization_barrier((value,) + earlier)[0]


NT = (((1,), (1,)), ((), ()))
TN = (((0,), (0,)), ((), ()))
WHOLE = pl.BlockSpec(memory_space=pltpu.VMEM)
SCRATCH = 14
QUICK = pl.CostEstimate(flops=1, bytes_accessed=1, transcendentals=0)


def params(mib):
    return pltpu.CompilerParams(vmem_limit_bytes=mib * 1024 * 1024)


def dot(a, b, dims=(((1,), (0,)), ((), ()))):
    return lax.dot_general(a, b, dims, preferred_element_type=jnp.float32)


def split(a):
    high = a.astype(jnp.bfloat16)
    return high, (a - high.astype(jnp.float32)).astype(jnp.bfloat16)


def place_kernel(experts, capacity, docs, tokens, routes, gates, doc, mask, filled, w_high, w_low, base):
    slots, count = w_high.shape
    features = tokens.shape[1]
    slot = lax.broadcasted_iota(jnp.int32, (slots, count), 0)
    expert = jnp.zeros((slots, count), jnp.int32)
    for e in range(1, experts):
        expert += (slot >= e * capacity).astype(jnp.int32)
    first = routes[0:1, :] == expert
    named = first | (routes[1:2, :] == expert)
    before = lax.broadcasted_iota(jnp.int32, (count, count), 0) < lax.broadcasted_iota(
        jnp.int32, (count, count), 1
    )
    one = jnp.float32(1)
    zero = jnp.float32(0)
    earlier = dot(
        jnp.where(named, one, zero).astype(jnp.bfloat16),
        jnp.where(before, one, zero).astype(jnp.bfloat16),
    )
    place = named & (earlier.astype(jnp.int32) == slot - expert * capacity)
    filled[:, :features] = dot(
        jnp.where(place, one, zero).astype(jnp.bfloat16), tokens[...]
    ).astype(jnp.bfloat16)
    weight = jnp.where(place, jnp.where(first, gates[0:1, :], gates[1:2, :]), zero)
    high, low = split(weight)
    w_high[...] = high
    w_low[...] = low
    lane_doc = lax.broadcasted_iota(jnp.int32, (LANES, count), 0)
    pooled = mask[...] == 1
    own = (doc[...] == lane_doc) & pooled & (lane_doc < docs)
    other = (doc[...] == lane_doc - docs) & pooled & (lane_doc < 2 * docs)
    own = jnp.where(own, one, zero)
    other = jnp.where(other, one, zero).astype(jnp.bfloat16)
    own_bf = own.astype(jnp.bfloat16)
    filled[:, features:] = (dot(high, own_bf, NT) + dot(low, other, NT)).astype(jnp.bfloat16)
    base[:, :features] = dot(own_bf[:docs], tokens[...])
    base[:, features:] = jnp.broadcast_to(
        jnp.sum(own[:docs], axis=1, keepdims=True), (docs, LANES)
    )


def place_tokens(tokens, routes, gates, doc, mask, experts, capacity, docs):
    count, features = tokens.shape
    slots = experts * capacity
    return pl.pallas_call(
        lambda *refs: place_kernel(experts, capacity, docs, *refs),
        out_specs=[WHOLE] * 4,
        out_shape=[
            jax.ShapeDtypeStruct((slots, features + LANES), jnp.bfloat16),
            jax.ShapeDtypeStruct((slots, count), jnp.bfloat16),
            jax.ShapeDtypeStruct((slots, count), jnp.bfloat16),
            jax.ShapeDtypeStruct((docs, features + LANES), jnp.float32),
        ],
        compiler_params=params(16),
        cost_estimate=QUICK,
    )(tokens, routes.T, gates.T, doc.reshape(1, count), mask.reshape(1, count))


def combine_kernel(tokens, w_high, w_low, returned, out):
    rows = returned[...]
    out[...] = (
        tokens[...].astype(jnp.float32) + dot(w_high[...], rows, TN) + dot(w_low[...], rows, TN)
    ).astype(jnp.bfloat16)


def combine(tokens, w_high, w_low, returned):
    return pl.pallas_call(
        combine_kernel,
        out_shape=jax.ShapeDtypeStruct(tokens.shape, jnp.bfloat16),
        compiler_params=params(16),
        cost_estimate=QUICK,
    )(tokens, w_high, w_low, returned)


def silu_times(gate, up):
    return (gate / (1.0 + jnp.exp(-gate)) * up).astype(jnp.bfloat16)


def experts_kernel(parts, pieces, adds, docs, *refs):
    xs = []
    for part in parts:
        xs.append(refs[:part])
        refs = refs[part:]
    count = len(parts)
    weights, refs = refs[: sum(pieces)], refs[sum(pieces) :]
    accs, refs = (refs[:count], refs[count:]) if adds else ([None] * count, refs)
    outs, sums_ref, pooled = refs[:-2], refs[-2], refs[-1]
    features = weights[0].shape[1]
    size = pieces[0]
    for group in range(count):
        x = jnp.concatenate([part[:, :features] for part in xs[group]], axis=0)
        shares = jnp.concatenate([part[:, features:] for part in xs[group]], axis=0)
        total = accs[group][...] if adds else None
        for piece in range(len(pieces)):
            gate, up = weights[size * piece], weights[size * piece + 1]
            hidden = silu_times(dot(x, gate[...], NT), dot(x, up[...], NT))
            found = dot(shares, hidden, TN)
            pooled[piece] = found if group == 0 else pooled[piece] + found
            if size == 2:
                outs[group * len(pieces) + piece][...] = hidden
                continue
            out = dot(hidden, weights[size * piece + 2][...])
            total = out if total is None else total + out
        if size > 2:
            outs[group][...] = total
    if size == 2:
        sums_ref[...] = pooled[...]
        return
    sums = jnp.zeros((docs, features), jnp.float32)
    for piece in range(len(pieces)):
        high, low = split(pooled[piece][:docs] + pooled[piece][docs : 2 * docs])
        down = weights[size * piece + 2][...]
        sums += dot(high, down) + dot(low, down)
    sums_ref[...] = sums


def run_experts(rows, pieces, docs, accs=None):
    weights = [w for piece in pieces for w in piece]
    block = sum(part.shape[0] for part in rows[0])
    width, features = weights[0].shape
    has_down = len(pieces[0]) > 2
    if has_down:
        out_shape = [jax.ShapeDtypeStruct((block, features), jnp.float32) for _ in rows]
        out_shape.append(jax.ShapeDtypeStruct((docs, features), jnp.float32))
    else:
        out_shape = [
            jax.ShapeDtypeStruct((block, width), jnp.bfloat16) for _ in rows for _ in pieces
        ]
        out_shape.append(jax.ShapeDtypeStruct((len(pieces), LANES, width), jnp.float32))
    operands = [part for group in rows for part in group] + [*weights, *(accs or [])]
    work = len(rows) * block * features * width * len(pieces)
    *outs, sums = pl.pallas_call(
        lambda *refs: experts_kernel(
            [len(r) for r in rows], [len(p) for p in pieces], accs is not None, docs, *refs
        ),
        in_specs=[WHOLE] * len(operands),
        out_specs=[WHOLE] * len(out_shape),
        out_shape=out_shape,
        scratch_shapes=[pltpu.VMEM((len(pieces), LANES, width), jnp.float32)],
        compiler_params=params(SCRATCH),
        cost_estimate=pl.CostEstimate(
            flops=work,
            bytes_accessed=sum(w.size for w in weights) // 4,
            transcendentals=len(rows) * block * width * len(pieces),
        ),
    )(*operands)
    return outs, sums


def add_downs_kernel(groups, pieces_parts, pooled_count, halves, docs, *refs):
    pieces = len(pieces_parts)
    hidden, refs = refs[: groups * pieces], refs[groups * pieces :]
    accs, refs = refs[:groups], refs[groups:]
    downs = []
    for parts in pieces_parts:
        downs.append(refs[:parts])
        refs = refs[parts:]
    pooled, refs = refs[:pooled_count], refs[pooled_count:]
    features = accs[0].shape[1]

    def product(a, piece):
        return jnp.concatenate([dot(a, part[...]) for part in downs[piece]], axis=1)

    if pooled_count:
        base, refs = refs[0], refs[1:]
        outs, sums_ref = refs[:-1], refs[-1]
        sums = base[:, :features]
        for piece in range(pieces):
            both = pooled[0][piece]
            for other in pooled[1:]:
                both = both + other[piece]
            high, low = split(both[:docs] + both[docs : 2 * docs])
            sums += product(high, piece) + product(low, piece)
        sums_ref[:, :features] = sums
        sums_ref[:, features:] = base[:, features:]
    else:
        outs = refs
    for group in range(groups):
        total = accs[group][...]
        for piece in range(pieces):
            total += product(hidden[group * pieces + piece][...], piece)
        if halves:
            half = total.shape[0] // 2
            outs[2 * group][...] = total[:half].astype(jnp.bfloat16)
            outs[2 * group + 1][...] = total[half:].astype(jnp.bfloat16)
        else:
            outs[group][...] = total.astype(outs[group].dtype)


def add_downs(hidden, accs, downs, docs, pooled=(), base=None, halves=False, dtype=jnp.bfloat16):
    block, features = accs[0].shape
    width = hidden[0][0].shape[1]
    if halves:
        out_shape = [
            jax.ShapeDtypeStruct((block // 2, features), dtype) for _ in range(2 * len(accs))
        ]
    else:
        out_shape = [jax.ShapeDtypeStruct((block, features), dtype) for _ in accs]
    operands = [h for group in hidden for h in group] + [*accs, *[part for down in downs for part in down], *pooled]
    if pooled:
        operands.append(base)
        out_shape.append(jax.ShapeDtypeStruct(base.shape, jnp.float32))
    return pl.pallas_call(
        lambda *refs: add_downs_kernel(
            len(accs), [len(down) for down in downs], len(pooled), halves, docs, *refs
        ),
        in_specs=[WHOLE] * len(operands),
        out_specs=[WHOLE] * len(out_shape),
        out_shape=out_shape,
        compiler_params=params(SCRATCH),
        cost_estimate=pl.CostEstimate(
            flops=len(accs) * block * features * width * len(downs) // 2,
            bytes_accessed=len(downs) * width * features // 4,
            transcendentals=0,
        ),
    )(*operands)


def add_parts_kernel(own, m_a, m_b, p_a, p_b, out):
    half = m_a.shape[0]
    for at, m, p in ((0, m_a, p_a), (half, m_b, p_b)):
        out[at : at + half, :] = (
            own[at : at + half, :].astype(jnp.float32)
            + m[...].astype(jnp.float32)
            + p[...].astype(jnp.float32)
        ).astype(jnp.bfloat16)


def add_parts(own, m_a, m_b, p_a, p_b):
    return pl.pallas_call(
        add_parts_kernel,
        in_specs=[WHOLE] * 5,
        out_specs=WHOLE,
        out_shape=jax.ShapeDtypeStruct(own.shape, jnp.bfloat16),
        compiler_params=params(SCRATCH),
        cost_estimate=QUICK,
    )(own, m_a, m_b, p_a, p_b)


def finish_kernel(features, first, own, one, two, three, part, loss):
    docs, share = part.shape
    total = (own[...] + two[...]) + (one[...] + three[...])
    means = total[:, :features] / jnp.maximum(total[:, features : features + 1], 1.0)
    part[...] = pltpu.roll(means, features - first[0], 1)[:, :share]
    products = lax.dot_general(
        means, means, NT, precision=lax.Precision.HIGHEST, preferred_element_type=jnp.float32
    )
    scale = lax.rsqrt(jnp.sum(means * means, axis=1, keepdims=True) / features + 1e-06)
    row = lax.broadcasted_iota(jnp.int32, (docs, docs), 0)
    column = lax.broadcasted_iota(jnp.int32, (docs, docs), 1)
    scale_of_column = jnp.sum(jnp.where(row == column, scale, 0.0), axis=0, keepdims=True)
    similarity = products * scale * scale_of_column / (features * SOFTMAX_TEMPER)
    odd = lax.rem(column, 2) == 1
    spread = jnp.sum(jnp.where(odd, jnp.exp(similarity), 0.0), axis=1, keepdims=True)
    matching = jnp.sum(jnp.where(column == row + 1, similarity, 0.0), axis=1, keepdims=True)
    even = lax.rem(lax.broadcasted_iota(jnp.int32, (docs, 1), 0), 2) == 0
    terms = jnp.where(even, jnp.log(spread) - matching, 0.0)
    loss[...] = jnp.sum(terms, axis=0, keepdims=True) / (docs // 2)


def finish(own, one, two, three, features, first, share):
    docs = own.shape[0]
    return pl.pallas_call(
        lambda *refs: finish_kernel(features, *refs),
        in_specs=[pl.BlockSpec(memory_space=pltpu.SMEM)] + [WHOLE] * 4,
        out_specs=[WHOLE] * 2,
        out_shape=[
            jax.ShapeDtypeStruct((docs, share), jnp.float32),
            jax.ShapeDtypeStruct((1, 1), jnp.float32),
        ],
        compiler_params=params(16),
        cost_estimate=QUICK,
    )(first, own, one, two, three)


def shards(tokens, w_gate, w_up, w_down, routes, gates, document_index, pool_mask):
    tok_count, feature_total = tokens.shape
    choose = routes.shape[1]
    expert_count = lax.axis_size("expert")
    section_count = lax.axis_size("section")
    side = math.isqrt(section_count)
    depth = expert_count // 2
    capacity = tok_count * choose * 5 // (4 * expert_count)
    slots = expert_count * capacity
    half_slots, half_features = slots // 2, feature_total // 2
    device_count = section_count * expert_count
    doc_count = 2 * (tok_count * device_count // DOC_LEN)

    def by_weight(a, step):
        return lax.ppermute(a, AXES, permutation(side, depth, (0, 1), step))

    def by_token(a, step):
        return lax.ppermute(a, AXES, permutation(side, depth, (1, 0), step))

    gate, up, down = w_gate[0].T, w_up[0].T, w_down[0]
    gate_p, gate_m = by_weight(gate, 1), by_weight(gate, -1)
    up_p, up_m = by_weight(up, 1), by_weight(up, -1)

    filled, w_high, w_low, base = place_tokens(
        tokens, routes, gates, document_index, pool_mask, expert_count, capacity, doc_count
    )
    mine = lax.all_to_all(
        filled.reshape(expert_count, capacity, -1), "expert", split_axis=0, concat_axis=0, tiled=True
    ).reshape(slots, -1)
    token_p, token_m = by_token(mine, 1), by_token(mine, -1)

    docs = doc_count
    own_piece = (gate, up, down)
    near_pieces = [(gate_p, up_p), (gate_m, up_m)]
    mine = after(mine, gate_p, gate_m, up_p, up_m)
    (acc_mine,), sums_0 = run_experts([(mine,)], [own_piece], docs)
    hidden_mine, pooled_0 = run_experts([(after(mine, sums_0),)], near_pieces, docs)
    down_late = after(down, gate_p, gate_m, up_p, up_m)
    down_p, down_m = by_weight(down_late, 1), by_weight(down_late, -1)
    token_p, token_m = lax.optimization_barrier((token_p, token_m, pooled_0))[:2]
    token_far = by_token(token_m, -1)
    (acc_p, acc_m), sums_1 = run_experts([(token_p,), (token_m,)], [own_piece], docs)
    (h_pp, h_pm, h_mp, h_mm), pooled_1 = run_experts(
        [(after(token_p, sums_1),), (token_m,)], near_pieces, docs
    )
    gate_far = by_weight(after(gate_p, pooled_0), 1)
    up_far = by_weight(after(up_m, pooled_0), -1)
    acc_p, acc_m, acc_mine, base = add_downs(
        [[h_pp, h_pm], [h_mp, h_mm], hidden_mine],
        [acc_p, acc_m, acc_mine],
        [(down_p,), (down_m,)],
        docs,
        pooled=[pooled_0, pooled_1],
        base=base,
        dtype=jnp.float32,
    )
    down_far = (by_weight(after(down_p, pooled_1), 1),)
    token_far = (after(token_far, base),)
    (acc_far,), sums_2 = run_experts(
        [token_far], [own_piece, (gate_p, up_p, down_p), (gate_m, up_m, down_m)], docs
    )
    base = jnp.concatenate(
        [base[:, :feature_total] + sums_0 + sums_1 + sums_2, base[:, feature_total:]], axis=1
    )

    far_piece = (after(gate_far, base), up_far)
    (h_far, h_mine), pooled_2 = run_experts([token_far, (mine,)], [far_piece], docs)
    out_far_a, out_far_b = add_downs([[h_far]], [acc_far], [down_far], docs, halves=True)
    far_a, far_b = by_token(out_far_a, -1), by_token(out_far_b, 1)
    (h_p, h_m), pooled_3 = run_experts(
        [(after(token_p, out_far_b),), (token_m,)], [far_piece], docs
    )
    out_p_a, out_p_b, out_m_a, out_m_b = add_downs(
        [[h_p], [h_m]], [acc_p, acc_m], [down_far], docs, halves=True
    )

    from_m_b = by_token(out_p_b, -1)
    from_p_a = by_token(out_m_a, 1)
    relay_m = (out_p_a.astype(jnp.float32) + far_a.astype(jnp.float32)).astype(jnp.bfloat16)
    relay_p = (out_m_b.astype(jnp.float32) + far_b.astype(jnp.float32)).astype(jnp.bfloat16)
    from_m_a, from_p_b = by_token(relay_m, -1), by_token(relay_p, 1)
    out_own, total = add_downs(
        [[after(h_mine, relay_m, relay_p)]],
        [acc_mine],
        [down_far],
        docs,
        pooled=[pooled_2, pooled_3],
        base=base,
        dtype=jnp.float32,
    )
    expert_out = add_parts(out_own, from_m_a, from_m_b, from_p_a, from_p_b)
    returned = lax.all_to_all(
        expert_out.reshape(expert_count, capacity, feature_total),
        "expert",
        split_axis=0,
        concat_axis=0,
        tiled=True,
    )
    moe_out = combine(tokens, w_high, w_low, returned.reshape(slots, feature_total))

    flip = [(i, i ^ 1) for i in range(device_count)]
    total = total + lax.ppermute(total, AXES, flip)
    pairs_z = lambda step: z_permutation(side, depth, step)
    pairs_t = lambda step: permutation(side, depth, (1, 0), step)
    pairs_w = lambda step: permutation(side, depth, (0, 1), step)
    for pairs_of in (pairs_z, pairs_t):
        one, two, three = (lax.ppermute(total, AXES, pairs_of(step)) for step in (1, 2, 3))
        total = (total + two) + (one + three)
    total = after(total, expert_out)
    one, two, three = (lax.ppermute(total, AXES, pairs_w(step)) for step in (1, 2, 3))
    share = feature_total // device_count
    first = (lax.axis_index(AXES) * share).astype(jnp.int32).reshape(1)
    emb_share, loss = finish(total, one, two, three, feature_total, first, share)
    return (moe_out, emb_share, loss[0, 0])


def solution(mesh):
    return jax.shard_map(
        shards,
        mesh=mesh,
        in_specs=(
            P(("section", "expert"), None),
            P("expert", None, "section"),
            P("expert", None, "section"),
            P("expert", "section", None),
            P(("section", "expert"), None),
            P(("section", "expert"), None),
            P(("section", "expert")),
            P(("section", "expert")),
        ),
        out_specs=(P(("section", "expert"), None), P(None, ("section", "expert")), P()),
        check_vma=False,
    )
```
